32 devices in a mesh: gx: 4 (over z), yz: 8 (over y, x, core).
Axes of the slice: x: 2, y: 2, z: 4, core: 2. Of those that a mesh axis runs over, the one named last changes fastest.
Arguments:
- fields: float32 [5, 256, 96, 512], P(None, 'yz', None, 'gx'), may hold values from -6 to 6
- inflow: float32 [5, 256, 96], P(None, 'yz'), may hold values from -6 to 6
- rates_fwd: float32 [256, 96, 512], P('yz', None, 'gx'), may hold values from 0.45 to 1
- rates_bwd: float32 [256, 96, 512], P('yz', None, 'gx'), may hold values from 0.45 to 1
- flux_wall: float32 [5, 5], replicated, may hold values from -2.5 to 2.5
- flux_span: float32 [5, 5], replicated, may hold values from -2.5 to 2.5
- viscosity: float32 [5], replicated, may hold values from 0.05 to 0.5
Outputs:
- advanced: float32 [5, 256, 96, 512], P(None, 'yz', None, 'gx')
The draws below stay inside these ranges and needn't reach their ends.
All inputs are finite; a program needn't handle non-finite values.
Results may differ from the reference program's by a relative error of at most 0.00018.
Values sent between devices are 32-bit elements; how exact they have to be, the bound alone decides.
No kernel may reach another device: no remote copies, remote signals or barrier semaphores. Data moves between devices by JAX's collectives and lax.ppermute only.
A program may use at most 256 MiB of HBM per device.

```python
import math
import jax
import jax.numpy as jnp
from jax import lax

FIELDS = 5
WALLWARD_NODES = 256
CROSSWISE_NODES = 96
CHORDWISE_BINS = 512


def make_rates(key):
    line_shape = (WALLWARD_NODES, CROSSWISE_NODES, 1)
    fast_share = 0.5
    fast_line = jax.random.uniform(jax.random.fold_in(key, 1), line_shape) < fast_share
    fast_len = jax.random.uniform(jax.random.fold_in(key, 2), line_shape, minval=30.0, maxval=50.0)
    slow_len = CHORDWISE_BINS * jnp.exp(jax.random.uniform(jax.random.fold_in(key, 3), line_shape, minval=math.log(4.0), maxval=math.log(16.0)))
    chord_extent = jnp.where(fast_line, fast_len, slow_len)
    wall_roughness_height = jax.random.uniform(jax.random.fold_in(key, 4), (WALLWARD_NODES, CROSSWISE_NODES, CHORDWISE_BINS), minval=0.5, maxval=2.0)
    pulse_hit_chance = jax.random.uniform(jax.random.fold_in(key, 5), (WALLWARD_NODES, CROSSWISE_NODES, CHORDWISE_BINS)) < 3.0 / CHORDWISE_BINS
    pulse_keep_factor = jax.random.uniform(jax.random.fold_in(key, 6), (WALLWARD_NODES, CROSSWISE_NODES, CHORDWISE_BINS), minval=0.5, maxval=0.8)
    damping_factors = jnp.exp(-wall_roughness_height / chord_extent) * jnp.where(pulse_hit_chance, pulse_keep_factor, 1.0)
    return damping_factors.astype(jnp.float32)


def draw_rates_fwd(key, part):
    return make_rates(jax.random.fold_in(key, 11))


def draw_rates_bwd(key, part):
    return make_rates(jax.random.fold_in(key, 23))


def block_levels(own_key, dims, shards, smallest, largest):
    level, own = 1.0, jax.random.fold_in(own_key, 6)
    for axis_at, shards_of in shards:
        heights = jnp.exp(jax.random.uniform(jax.random.fold_in(own, axis_at), (shards_of,), jnp.float32, smallest / len(shards), largest / len(shards)))
        level = level * jnp.repeat(heights, dims[axis_at] // shards_of).reshape([-1 if axis == axis_at else 1 for axis in range(len(dims))])
    return level


def normal_values(own_key, dims, spread, limit, pieces=(), dtype=jnp.bfloat16):
    gain = block_levels(own_key, dims, pieces, -0.22, 0.18) if pieces else 1.0
    drawn = jax.random.normal(own_key, dims, jnp.float32) * spread * gain
    return jnp.minimum(jnp.maximum(drawn, -limit), limit).astype(dtype)


def setup_inputs(seed: int = 0) -> dict:
    seeds = jax.random.split(jax.random.key(seed), 8)
    return {
        "fields": normal_values(seeds[0], (FIELDS, WALLWARD_NODES, CROSSWISE_NODES, CHORDWISE_BINS), 1.0, 6.0, ((1, 8), (3, 4)), jnp.float32),
        "inflow": normal_values(seeds[1], (FIELDS, WALLWARD_NODES, CROSSWISE_NODES), 1.0, 6.0, ((1, 8),), jnp.float32),
        "rates_fwd": draw_rates_fwd(jax.random.fold_in(seeds[7], 71), 0),
        "rates_bwd": draw_rates_bwd(jax.random.fold_in(seeds[7], 71), 0),
        "flux_wall": normal_values(seeds[4], (FIELDS, FIELDS), FIELDS ** -0.5, 2.5, (), jnp.float32),
        "flux_span": normal_values(seeds[5], (FIELDS, FIELDS), FIELDS ** -0.5, 2.5, (), jnp.float32),
        "viscosity": jnp.clip(jnp.exp(jax.random.uniform(seeds[6], (FIELDS,), jnp.float32, math.log(0.05), math.log(0.5))), 0.05, 0.5),
    }


ALPHA_D = 0.25
ALPHA_F = 0.499
TIME_STEP = 0.5

def root_of(coupling):
    return (-1.0 + math.sqrt(1.0 - 4.0 * coupling * coupling)) / (2.0 * coupling)

def signed_power(exponent, ratio):
    magnitude = jnp.exp(exponent.astype(jnp.float32) * math.log(abs(ratio)))
    parity = jnp.where(exponent % 2 == 0, 1.0, -1.0).astype(jnp.float32)
    return magnitude * parity

def inverse_of(points, coupling, periodic):
    ratio = root_of(coupling)
    row_idx = lax.broadcasted_iota(jnp.int32, (points, points), 0)
    col_idx = lax.broadcasted_iota(jnp.int32, (points, points), 1)
    if periodic:
        offset = (col_idx - row_idx) % points
        factor = 1.0 / ((1.0 + 2.0 * coupling * ratio) * (1.0 - ratio ** points))
        return factor * (signed_power(offset, ratio) + signed_power(points - offset, ratio))
    near_idx = jnp.minimum(row_idx, col_idx)
    far_idx = jnp.maximum(row_idx, col_idx)
    factor = 1.0 / ((1.0 + 2.0 * coupling * ratio) * (1.0 - ratio ** (2 * points + 2)))
    numerator = signed_power(far_idx - near_idx, ratio) * (1.0 - signed_power(2 * near_idx + 2, ratio))
    numerator = numerator * (1.0 - signed_power(2 * points - 2 * far_idx, ratio))
    return factor * numerator

def band_of(points, below, centre, above, periodic):
    row_idx = lax.broadcasted_iota(jnp.int32, (points, points), 0)
    col_idx = lax.broadcasted_iota(jnp.int32, (points, points), 1)
    offset = col_idx - row_idx
    if periodic:
        offset = (offset + 1) % points - 1
    values = jnp.where(offset == 0, centre, jnp.where(offset == 1, above, jnp.where(offset == -1, below, 0.0)))
    return values.astype(jnp.float32)

def operators(points, periodic):
    highest = lax.Precision.HIGHEST
    deriv_op = jnp.dot(inverse_of(points, ALPHA_D, periodic), band_of(points, -0.75, 0.0, 0.75, periodic), precision=highest)
    half_side = 0.5 * (0.5 + ALPHA_F)
    filter_op = jnp.dot(inverse_of(points, ALPHA_F, periodic), band_of(points, half_side, 0.5 + ALPHA_F, half_side, periodic), precision=highest)
    deriv_filter = jnp.dot(deriv_op, filter_op, precision=highest)
    second_filter = jnp.dot(deriv_op, deriv_filter, precision=highest)
    return jnp.stack([filter_op, deriv_filter, second_filter])

def mix_fields(matrix, values):
    return jnp.einsum('fg,gyzx->fyzx', matrix, values, precision=lax.Precision.HIGHEST)

def compose(earlier, later):
    gain_early, sum_early = earlier
    gain_late, sum_late = later
    return (gain_early * gain_late, gain_late * sum_early + sum_late)

def reference(fields, inflow, rates_fwd, rates_bwd, flux_wall, flux_span, viscosity):
    highest = lax.Precision.HIGHEST
    span_ops = operators(CROSSWISE_NODES, True)
    wall_ops = operators(WALLWARD_NODES, False)
    along_z = jnp.einsum('kab,fybx->kfyax', span_ops, fields, precision=highest)
    along_y = jnp.einsum('kab,fbzx->kfazx', wall_ops, along_z[0], precision=highest)
    span_first = jnp.einsum('ab,fbzx->fazx', wall_ops[0], along_z[1], precision=highest)
    span_second = jnp.einsum('ab,fbzx->fazx', wall_ops[0], along_z[2], precision=highest)
    visc_col = viscosity[:, None, None, None]
    right_side = along_y[0] + TIME_STEP * (-mix_fields(flux_wall, along_y[1]) - mix_fields(flux_span, span_first) + visc_col * (along_y[2] + span_second))
    fwd_gain = jnp.broadcast_to(rates_fwd, right_side.shape)
    fwd_prod, fwd_sum = lax.associative_scan(compose, (fwd_gain, (1.0 - rates_fwd) * right_side), axis=3)
    forward = fwd_prod * inflow[..., None] + fwd_sum
    x_index = lax.broadcasted_iota(jnp.int32, rates_bwd.shape, 2)
    bwd_rate = jnp.where(x_index == CHORDWISE_BINS - 1, 0.0, rates_bwd)
    bwd_gain = jnp.broadcast_to(bwd_rate, right_side.shape)
    bwd_prod, bwd_sum = lax.associative_scan(compose, (bwd_gain, (1.0 - bwd_rate) * forward), reverse=True, axis=3)
    return bwd_sum
```

```python
import functools

import jax
import jax.numpy as jnp
import numpy as np
from jax import lax
from jax.experimental import pallas as pl
from jax.experimental.pallas import tpu as pltpu
from jax.sharding import PartitionSpec as P

F32, BF16 = jnp.float32, jnp.bfloat16
STEP = 0.5
LIMITS = {"mats": 56, "taps": 56, "chip": 8, "span": 12, "rates": 12, "states": 10, "sweep": 56, "close": 56}


def tridiagonal(points, below, centre, above, periodic):
    band = centre * np.eye(points) + below * np.eye(points, k=-1) + above * np.eye(points, k=1)
    if periodic:
        band[0, -1] += below
        band[-1, 0] += above
    return band


def operators(points, periodic):
    deriv = np.linalg.solve(
        tridiagonal(points, 0.25, 1.0, 0.25, periodic),
        tridiagonal(points, -0.75, 0.0, 0.75, periodic),
    )
    smooth = np.linalg.solve(
        tridiagonal(points, 0.499, 1.0, 0.499, periodic),
        tridiagonal(points, 0.4995, 0.999, 0.4995, periodic),
    )
    return smooth, deriv @ smooth, deriv @ deriv @ smooth


def wall_tables(points, devs):
    ops = operators(points, False)
    rows = points // devs

    def frame(first):
        vecs = np.stack(first)
        basis = []
        for vec in vecs:
            for _ in range(3):
                for other in basis:
                    vec = vec - other * (other @ vec)
            basis.append(vec / np.linalg.norm(vec))
        return np.stack(basis)

    above, below = {}, {}
    for edge in range(rows, points, rows):
        above[edge] = np.zeros((3, points))
        above[edge][:, edge:] = frame([op[edge - 1, edge:] for op in ops])
        below[edge] = np.zeros((3, points))
        below[edge][:, :edge] = frame([op[edge, :edge] for op in ops])
    nothing = np.zeros((3, points))
    above_at = lambda edge: above.get(edge, nothing)
    below_at = lambda edge: below.get(edge, nothing)

    def carry_above(target, source):
        return above_at(target) @ above_at(source).T

    def carry_below(target, source):
        return below_at(target) @ below_at(source).T

    chips = devs // 2
    taps = np.zeros((devs, 6, rows))
    local = np.zeros((devs, 3, rows, rows))
    reach = np.zeros((devs, 3, rows, 6))
    chip_mix = np.zeros((devs, 2, 3, 6))
    from_chip = np.zeros((devs, 2, max(chips - 1, 1), 3, 3))
    to_core = np.zeros((devs, 4, 3, 3))
    eye = np.eye(3)
    for dev in range(devs):
        low, high = dev * rows, (dev + 1) * rows
        own = slice(low, high)
        taps[dev, :3] = above_at(low)[:, own]
        taps[dev, 3:] = below_at(high)[:, own]
        for at, op in enumerate(ops):
            local[dev, at] = op[own, own]
            reach[dev, at, :, :3] = op[own] @ above_at(high).T
            reach[dev, at, :, 3:] = op[own] @ below_at(low).T
        chip, core = divmod(dev, 2)
        start, middle, end = 2 * chip * rows, (2 * chip + 1) * rows, (2 * chip + 2) * rows
        up = [eye, carry_above(start, middle)]
        down = [carry_below(end, middle), eye]
        chip_mix[dev, 0] = np.concatenate([up[core], up[1 - core]], 1)
        chip_mix[dev, 1] = np.concatenate([down[core], down[1 - core]], 1)
        for at in range(1, chips):
            other = chip ^ at
            if other > chip:
                from_chip[dev, 0, at - 1] = carry_above(end, 2 * other * rows)
            else:
                from_chip[dev, 1, at - 1] = carry_below(start, (2 * other + 2) * rows)
        above_core = [carry_above(middle, end), eye]
        below_core = [eye, carry_below(middle, start)]
        to_core[dev, 0], to_core[dev, 1] = above_core[core], above_core[1 - core]
        to_core[dev, 2], to_core[dev, 3] = below_core[core], below_core[1 - core]
    return taps, local, reach, chip_mix, from_chip, to_core


def wall_layout(local, reach, fields):
    devs, _, rows, _ = local.shape
    states = reach.transpose(0, 1, 3, 2)
    us = -(-6 * fields // 32) * 32
    ws = -(-(2 * fields * rows + us + 2 * fields) // 128) * 128 - 2 * fields * rows - us
    width = 2 * fields * rows + us + ws
    owner = np.full(width, -1)
    parts = np.zeros((devs, 3, rows, width))
    for field in range(fields):
        at = slice(field * rows, (field + 1) * rows)
        owner[at] = field
        parts[:, 1:, :, at] = local[:, 1:]
        at = slice(fields * rows + us + field * rows, fields * rows + us + (field + 1) * rows)
        owner[at] = field
        parts[:, 0, :, at] = local[:, 0]
        for k in range(6):
            at = fields * rows + k * fields + field
            owner[at] = field
            parts[:, 1:, :, at] = states[:, 1:, k]
        for place, k in enumerate((0, 3)):
            at = 2 * fields * rows + us + place * fields + field
            owner[at] = field
            parts[:, 0, :, at] = states[:, 0, k]
    pick = (owner[None] == np.arange(fields)[:, None]).astype(np.float64)
    tall = np.concatenate([parts] * fields, axis=2)
    same = np.repeat(pick, rows, axis=0)
    return tall[:, 1:], tall[:, 0] * same, pick, us, ws


def split(value):
    high = np.asarray(value, np.float32).astype(BF16)
    low = (np.asarray(value, np.float32) - high.astype(np.float32)).astype(BF16)
    return np.concatenate([high, high, low], axis=-1)


def parted(value):
    high = value.astype(BF16)
    return high, (value - high.astype(F32)).astype(BF16)


def dot(a, b):
    return jnp.dot(a, b, preferred_element_type=F32)


def stacked(value):
    high, low = parted(value)
    return jnp.concatenate([high, low, high], axis=0)


def padded(value, to):
    if value.shape[0] == to:
        return value
    return jnp.concatenate([value, jnp.zeros((to - value.shape[0], value.shape[1]), F32)], axis=0)


def running(value, twice):
    high, low = parted(value)
    return dot(jnp.concatenate([high, low], axis=1), twice)


def mats_kernel(fields, flux_wall_ref, flux_span_ref, visc_ref, wall_rows_ref, wall_cols_ref,
                wall_ref, wall_plain_ref, span_rows_ref, span_cols_ref, span_ref, span_plain_ref,
                wall_out, span_out):
    exact = functools.partial(jnp.dot, precision=lax.Precision.HIGHEST, preferred_element_type=F32)
    size = visc_ref.shape[1]
    here = lax.broadcasted_iota(jnp.int32, (size, size), 0) == lax.broadcasted_iota(
        jnp.int32, (size, size), 1)
    visc = jnp.where(here, STEP * visc_ref[...], 0.0)
    for flux_ref, rows_ref, cols_ref, ops, plain, out in (
        (flux_wall_ref, wall_rows_ref, wall_cols_ref, wall_ref[0], wall_plain_ref[0], wall_out),
        (flux_span_ref, span_rows_ref, span_cols_ref, span_ref[...], span_plain_ref[...], span_out),
    ):
        rows, cols = rows_ref[...], cols_ref[...]
        first = exact(exact(rows, -STEP * flux_ref[...]), cols)
        second = exact(exact(rows, visc), cols)
        high, low = parted(first * ops[0] + second * ops[1] + plain)
        width = cols.shape[1]
        out[:, :width] = high
        out[:, width : 2 * width] = high
        out[:, 2 * width :] = low


def mats_kernel_at(fields, dev_ref, *refs):
    mats_kernel(fields, *refs)


def taps_kernel(taps_ref, x_ref, keep_ref, send_ref):
    rows = x_ref.shape[1]
    me = lax.axis_index("yz")
    base = me * (6 * rows)
    half = x_ref.shape[2] // 2
    step = half if half <= 48 else 8
    core = me % 2
    for out_ref, offset in ((keep_ref, core * half), (send_ref, (1 - core) * half)):

        def piece(at, _):
            source = pl.multiple_of(offset + at * step, 8)
            sums = [None] * 6
            for row in range(rows):
                value = x_ref[0, row, pl.ds(source, step), :]
                for tap in range(6):
                    term = taps_ref[base + (tap * rows + row)] * value
                    sums[tap] = term if row == 0 else sums[tap] + term
            for tap in range(6):
                out_ref[tap, 0, pl.ds(pl.multiple_of(at * step, 8), step), :] = sums[tap]
            return 0

        lax.fori_loop(0, half // step, piece, 0)


def chip_kernel(chips, mix_ref, own_ref, other_ref, *out_refs):
    me = lax.axis_index("yz")
    chip, base = me // 2, me * 36
    lines = own_ref.shape[1]

    def piece(at, _):
        span = pl.ds(pl.multiple_of(at * 24, 8), 24)
        sums = []
        for side in range(2):
            terms = [own_ref[3 * side + k, span, :] for k in range(3)]
            terms += [other_ref[3 * side + k, span, :] for k in range(3)]
            sums.append(
                [sum(mix_ref[base + (18 * side + 6 * row + k)] * terms[k] for k in range(6)) for row in range(3)]
            )
        for at_chip in range(1, chips):
            lower = chip < (chip ^ at_chip)
            for row in range(3):
                out_refs[at_chip - 1][row, span, :] = jnp.where(lower, sums[1][row], sums[0][row])
        return 0

    lax.fori_loop(0, lines // 24, piece, 0)


def states_kernel(chips, from_ref, to_ref, own_ref, other_ref, *refs):
    me = lax.axis_index("yz")
    core, from_base, to_base = me % 2, me * (18 * (chips - 1)), me * 36
    arrived, (mine_ref, theirs_ref) = refs[: chips - 1], refs[chips - 1 :]
    lines = own_ref.shape[1]

    def piece(at, _):
        span = pl.ds(pl.multiple_of(at * 24, 8), 24)
        for side in range(2):
            into = [jnp.zeros((24, own_ref.shape[2]), F32) for _ in range(3)]
            for at_chip in range(chips - 1):
                for k in range(3):
                    value = arrived[at_chip][k, span, :]
                    for row in range(3):
                        into[row] += from_ref[from_base + (9 * (side * (chips - 1) + at_chip) + 3 * row + k)] * value
            for_mine = (core == 0) if side == 0 else (core == 1)
            for row in range(3):
                to_mine = sum(to_ref[to_base + (18 * side + 3 * row + k)] * into[k] for k in range(3))
                to_theirs = sum(to_ref[to_base + (18 * side + 9 + 3 * row + k)] * into[k] for k in range(3))
                near = 3 * side + row
                mine_ref[near, span, :] = to_mine + jnp.where(for_mine, other_ref[near, span, :], 0.0)
                theirs_ref[near, span, :] = to_theirs + jnp.where(
                    for_mine, 0.0, own_ref[near, span, :]
                )
        return 0

    lax.fori_loop(0, lines // 24, piece, 0)


def span_kernel(smooth_ref, mixed_ref, x_ref, smooth_out, mixed_out):
    fields, pair, span, cells = x_ref.shape
    wide = jnp.concatenate([x_ref[:, row].reshape(fields * span, cells) for row in range(pair)], 1)
    mixed = dot(mixed_ref[...], stacked(padded(wide, mixed_ref.shape[1] // 3)))
    for field in range(fields):
        part = slice(field * span, (field + 1) * span)
        smooth = dot(smooth_ref[...], stacked(wide[part]))
        for row in range(pair):
            place = slice(row * cells, (row + 1) * cells)
            smooth_out[field, row] = smooth[:, place]
            mixed_out[field, row] = mixed[part, place]


def rates_kernel(last_ref, logs_ref, sums_ref, ends_ref, fwd_ref, bwd_ref, *outs):
    win_ref, rf_ref, wout_ref, rb_ref, carry_ref, tail_ref, gains_ref = outs
    rows, span, cells = fwd_ref.shape

    def gathered(rate, mat):
        value = jnp.log(rate)
        high = value.astype(BF16)
        rest = value - high.astype(F32)
        middle = rest.astype(BF16)
        low = (rest - middle.astype(F32)).astype(BF16)
        terms = jnp.concatenate([high, middle, low], axis=1)
        both = dot(terms, mat)
        return both[:, :cells], both[:, cells:], terms

    def across(which, terms):
        mat = ends_ref[which][:, : terms.shape[1]]
        return [lax.dot_general(mat, terms[row * span : (row + 1) * span], (((1,), (1,)), ((), ())),
                                preferred_element_type=F32) for row in range(rows)]

    fwd = fwd_ref[...].reshape(rows * span, cells)
    bwd = bwd_ref[...].reshape(rows * span, cells)
    lane = lax.broadcasted_iota(jnp.int32, fwd.shape, 1)
    relative, absolute, terms = gathered(fwd, logs_ref[0])
    fwd_ends = across(0, terms)
    win_ref[...] = ((1.0 - fwd) * jnp.exp(-relative)).reshape(rows, span, cells)
    rf_ref[...] = jnp.exp(relative).reshape(rows, span, cells)
    entered = jnp.exp(absolute)
    relative, absolute, terms = gathered(bwd, logs_ref[1])
    bwd_ends = across(1, terms)
    grow = jnp.exp(relative)
    keep = jnp.where((lane == cells - 1) & (last_ref[0] == 1), 1.0, 1.0 - bwd)
    weight = keep * jnp.exp(-relative)
    wout_ref[...] = weight.reshape(rows, span, cells)
    rb_ref[...] = grow.reshape(rows, span, cells)
    tail_ref[...] = jnp.exp(absolute).reshape(rows, span, cells)
    high, low = parted(entered * weight)
    terms = jnp.concatenate([high, low], axis=1)
    carry_ref[...] = (grow * dot(terms, sums_ref[...])).reshape(rows, span, cells)
    carry_ends = across(2, terms)
    gains_ref[...] = jnp.zeros_like(gains_ref)
    for row in range(rows):
        ends_f, ends_b = jnp.exp(fwd_ends[row]), jnp.exp(bwd_ends[row])
        gains = (ends_f[0:1], ends_b[0:1], carry_ends[row][0:1] * ends_b[1:2], ends_f[1:2],
                 ends_b[1:2])
        for at, gain in enumerate(gains):
            gains_ref[at, row, :, :span] = gain


def sweep_kernel(rows, smooth_ref, mixed_ref, wall_ref, sums_ref, mine_ref,
                 recv_ref, u_ref, w_ref, win_ref, rf_ref, wout_ref, rb_ref, out_ref, last_ref,
                 first_ref, us_ref, ws_ref):
    tile = u_ref.shape[1]
    cells = u_ref.shape[2]
    fields, half = mine_ref.shape[1], mine_ref.shape[2]
    span = 2 * half
    lines = fields * rows
    at = pl.program_id(0)

    @pl.when(at == 0)
    def _():
        us_ref[pl.ds(6 * fields * span, us_ref.shape[0] - 6 * fields * span), :] = jnp.zeros(
            (us_ref.shape[0] - 6 * fields * span, cells), F32)
        ws_ref[pl.ds(2 * fields * span, ws_ref.shape[0] - 2 * fields * span), :] = jnp.zeros(
            (ws_ref.shape[0] - 2 * fields * span, cells), F32)
        last_ref[...] = jnp.zeros_like(last_ref)
        first_ref[...] = jnp.zeros_like(first_ref)
        first_core = lax.axis_index("yz") % 2 == 0

        def state(k):
            mine, recv = mine_ref[k], recv_ref[k]
            both = [jnp.where(first_core, mine, recv), jnp.where(first_core, recv, mine)]
            return jnp.concatenate(both, axis=1).reshape(fields * span, cells)

        for pair in ((0, 3), (1, 2), (4, 5)):
            wide = jnp.concatenate([state(k) for k in pair], axis=1)
            for field in range(fields):
                part = slice(field * span, (field + 1) * span)
                smooth = dot(smooth_ref[...], stacked(wide[part]))
                for place, k in enumerate(pair):
                    us_ref[pl.ds((k * fields + field) * span, span), :] = smooth[
                        :, place * cells : (place + 1) * cells
                    ]
            if pair == (0, 3):
                mixed = dot(mixed_ref[...], stacked(padded(wide, mixed_ref.shape[1] // 3)))
                for place in range(2):
                    ws_ref[pl.ds(place * fields * span, fields * span), :] = mixed[
                        :, place * cells : (place + 1) * cells
                    ]

    u_flat = u_ref.reshape(lines * tile, cells)
    w_flat = w_ref.reshape(lines * tile, cells)
    out_flat = out_ref.reshape(lines * tile, cells)
    rate_flat = [ref.reshape(rows * tile, cells) for ref in (win_ref, rf_ref, wout_ref, rb_ref)]
    lane = lax.broadcasted_iota(jnp.int32, (lines, last_ref.shape[1]), 1)
    last, first = last_ref[...], first_ref[...]
    rates = [
        jnp.concatenate([
            value for z in range(tile) for value in [ref[pl.ds(z, rows, stride=tile), :]] * fields], 0)
        for ref in rate_flat
    ]
    rights = []
    for z in range(0, tile, 2):
        wide = []
        for zz in (z, z + 1):
            where = at * tile + zz
            wide.append(jnp.concatenate([
                u_flat[pl.ds(zz, lines, stride=tile), :],
                us_ref[pl.ds(where, us_ref.shape[0] // span, stride=span), :],
                w_flat[pl.ds(zz, lines, stride=tile), :],
                ws_ref[pl.ds(where, ws_ref.shape[0] // span, stride=span), :]], 0))
        right = dot(wall_ref[...], stacked(jnp.concatenate(wide, 1)))
        rights += [right[:, :cells], right[:, cells:]]
    ahead = running(jnp.concatenate(rights, 0) * rates[0], sums_ref[0])
    ahead, total = ahead[:, :cells] * rates[1], ahead[:, cells:]
    result = running(ahead * rates[2], sums_ref[1])
    result, total_back = result[:, :cells] * rates[3], result[:, cells:]
    for z in range(tile):
        part = slice(z * lines, (z + 1) * lines)
        here = lane == at * tile + z
        out_flat[pl.ds(z, lines, stride=tile), :] = result[part]
        last = jnp.where(here, total[part], last)
        first = jnp.where(here, total_back[part], first)
    last_ref[...] = last
    first_ref[...] = first


def close_kernel(carry_ref, tail_ref, enter_ref, back_ref, t_ref, out_ref):
    fields, rows, span, _ = t_ref.shape
    for field in range(fields):
        enter = enter_ref[field].T[:span]
        back = back_ref[field].T[:span]
        for row in range(rows):
            out_ref[field, row] = (
                t_ref[field, row]
                + carry_ref[row] * enter[:, row : row + 1]
                + tail_ref[row] * back[:, row : row + 1]
            )


def params(limit):
    return pltpu.CompilerParams(vmem_limit_bytes=limit * 2**20)


def cost(flops, moved):
    return pl.CostEstimate(flops=int(flops), bytes_accessed=int(moved), transcendentals=0)


def whole(memory=pltpu.VMEM):
    return pl.BlockSpec(memory_space=memory)


SMEM = whole(pltpu.SMEM)


def shards(fields, inflow, rates_fwd, rates_bwd, flux_wall, flux_span, viscosity):
    n_fields, rows, span, cells = fields.shape
    devs, sections = lax.axis_size("yz"), lax.axis_size("gx")
    me, section = lax.axis_index("yz"), lax.axis_index("gx")
    chips, half = devs // 2, span // 2
    lines = n_fields * rows
    taps, local, reach, *maps = wall_tables(rows * devs, devs)
    flat = lambda table: jnp.asarray(np.asarray(table, np.float32).reshape(-1))
    taps, chip_mix, from_chip, to_core = (flat(table) for table in (taps, *maps))
    f32 = lambda table: jnp.asarray(np.asarray(table, np.float32))
    span_ops = operators(span, True)
    wall_ops, wall_plain, wall_pick, n_us, n_ws = wall_layout(local, reach, n_fields)
    width = wall_pick.shape[1]
    span_width = -(-n_fields * span // 128) * 128
    pad = lambda mat: np.pad(mat, [(0, 0)] * (mat.ndim - 1) + [(0, span_width - n_fields * span)])
    size = 8
    pick_rows = lambda count: np.pad(
        np.repeat(np.eye(n_fields), count, axis=0), ((0, 0), (0, size - n_fields)))
    span_cols = np.pad(pad(np.repeat(np.eye(n_fields), span, axis=1)), ((0, size - n_fields), (0, 0)))
    wall_cols = np.pad(wall_pick, ((0, size - n_fields), (0, 0)))
    square = lambda mat: jnp.pad(mat, ((0, size - n_fields), (0, size - n_fields)))
    smooth_mat = jnp.asarray(split(span_ops[0]))
    dev_block = lambda *shape: pl.BlockSpec(
        (1, *shape), lambda i, dev: (dev[0],) + (0,) * len(shape))
    full_block = lambda *shape: pl.BlockSpec(shape, lambda i, dev: (0,) * len(shape))
    all_span = n_fields * span
    wall_mat, mixed_mat = pl.pallas_call(
        functools.partial(mats_kernel_at, n_fields),
        grid_spec=pltpu.PrefetchScalarGridSpec(
            num_scalar_prefetch=1,
            grid=(1,),
            in_specs=[
                full_block(size, size), full_block(size, size), full_block(1, size),
                full_block(lines, size), full_block(size, width), dev_block(2, lines, width),
                dev_block(lines, width), full_block(all_span, size), full_block(size, span_width),
                full_block(2, all_span, span_width), full_block(all_span, span_width)],
            out_specs=[full_block(lines, 3 * width), full_block(all_span, 3 * span_width)],
        ),
        out_shape=[
            jax.ShapeDtypeStruct((lines, 3 * width), BF16),
            jax.ShapeDtypeStruct((all_span, 3 * span_width), BF16)],
        compiler_params=params(LIMITS["mats"]),
        cost_estimate=cost(10**7, 8 * 10**6),
        name="mats",
    )(me.astype(jnp.int32).reshape(1), square(flux_wall), square(flux_span),
      jnp.pad(viscosity, (0, size - n_fields)).reshape(1, size), f32(pick_rows(rows)),
      f32(wall_cols), f32(wall_ops), f32(wall_plain), f32(pick_rows(span)), f32(span_cols),
      f32(np.stack([pad(np.tile(op, (n_fields, n_fields))) for op in span_ops[1:]])),
      f32(pad(np.kron(np.eye(n_fields), span_ops[0]))))
    tri = np.triu(np.ones((cells, cells), np.float32))
    ones = np.ones_like(tri)
    twice = lambda mat: np.concatenate([mat, mat], 0)
    sums = jnp.asarray(np.stack([
        twice(np.concatenate([tri, ones], 1)), twice(np.concatenate([tri.T, ones], 1))
    ])).astype(BF16)
    logs_fwd = tri - tri[:, cells // 2 - 1 :][:, :1]
    logs_bwd = tri.T - tri.T[:, cells // 2 :][:, :1]
    thrice = lambda mat: np.concatenate([mat, mat, mat], 0)
    logs = jnp.asarray(np.stack([
        thrice(np.concatenate([logs_fwd, tri], 1)), thrice(np.concatenate([logs_bwd, tri.T], 1))
    ])).astype(BF16)

    tap_shape = jax.ShapeDtypeStruct((6, n_fields, half, cells), F32)
    tap_block = pl.BlockSpec((6, 1, half, cells), lambda f: (0, f, 0, 0))
    keep, send = pl.pallas_call(
        taps_kernel,
        grid=(n_fields,),
        in_specs=[SMEM, pl.BlockSpec((1, rows, span, cells), lambda f: (f, 0, 0, 0))],
        out_specs=[tap_block, tap_block],
        out_shape=[tap_shape, tap_shape],
        compiler_params=params(LIMITS["taps"]),
        cost_estimate=cost(12 * fields.size, 4 * fields.size),
        name="taps",
    )(taps, fields)
    swap_cores = [(dev, dev ^ 1) for dev in range(devs)]
    tap_lines = n_fields * half
    keep = keep.reshape(6, tap_lines, cells)
    other = lax.ppermute(send.reshape(6, tap_lines, cells), "yz", swap_cores)
    part_shape = jax.ShapeDtypeStruct((3, tap_lines, cells), F32)
    outgoing = pl.pallas_call(
        functools.partial(chip_kernel, chips),
        in_specs=[SMEM, whole(), whole()],
        out_specs=[whole()] * (chips - 1),
        out_shape=[part_shape] * (chips - 1),
        compiler_params=params(LIMITS["chip"]),
        cost_estimate=cost(6 * keep.size, 12 * keep.size),
        name="chip",
    )(chip_mix, keep, other)
    held_fields, held_fwd, held_bwd, wall_mat, mixed_mat, *outgoing = lax.optimization_barrier(
        (fields, rates_fwd, rates_bwd, wall_mat, mixed_mat, *outgoing))
    arrived = [
        lax.ppermute(value, "yz", [(dev, dev ^ (2 * (at + 1))) for dev in range(devs)])
        for at, value in enumerate(outgoing)
    ]
    pair_block = pl.BlockSpec((n_fields, 2, span, cells), lambda i: (0, i, 0, 0))
    field_shape = jax.ShapeDtypeStruct(fields.shape, F32)
    smooth, mixed = pl.pallas_call(
        span_kernel,
        grid=(rows // 2,),
        in_specs=[whole(), whole(), pair_block],
        out_specs=[pair_block, pair_block],
        out_shape=[pltpu.HBM(fields.shape, F32)] * 2,
        compiler_params=params(LIMITS["span"]),
        cost_estimate=cost(2 * 4000 * fields.size, 12 * fields.size),
        name="span",
    )(smooth_mat, mixed_mat, held_fields)

    n_rate = 4
    rate_block = pl.BlockSpec((n_rate, span, cells), lambda i: (i, 0, 0))
    rate_shape = jax.ShapeDtypeStruct(rates_fwd.shape, F32)
    is_last = (section == sections - 1).astype(jnp.int32).reshape(1)
    lanes = -(-span // 128) * 128
    widen = lambda value: jnp.pad(value, [(0, 0)] * (value.ndim - 1) + [(0, lanes - span)])
    ends = np.zeros((3, 16, 3 * cells))
    ends[:, 0] = 1.0
    ends[0, 1] = np.tile(np.arange(cells) >= cells // 2, 3)
    ends[1, 1] = np.tile(np.arange(cells) < cells // 2, 3)
    *rate_parts, carry, tail, gains = pl.pallas_call(
        rates_kernel,
        grid=(rows // n_rate,),
        in_specs=[SMEM, whole(), whole(), whole(), rate_block, rate_block],
        out_specs=[rate_block] * 6 + [pl.BlockSpec((5, n_rate, 1, lanes), lambda i: (0, i, 0, 0))],
        out_shape=[pltpu.HBM(rates_fwd.shape, F32)] * 6 + [jax.ShapeDtypeStruct((5, rows, 1, lanes), F32)],
        compiler_params=params(LIMITS["rates"]),
        cost_estimate=cost(2 * 4000 * rates_fwd.size, 32 * rates_fwd.size),
        name="rates",
    )(is_last, logs, sums[1, :, :cells], jnp.asarray(ends.astype(BF16)), held_fwd, held_bwd)
    smooth, mixed, gains, *arrived = lax.optimization_barrier((smooth, mixed, gains, *arrived))
    six_shape = jax.ShapeDtypeStruct((6, tap_lines, cells), F32)
    mine, theirs = pl.pallas_call(
        functools.partial(states_kernel, chips),
        in_specs=[SMEM] * 2 + [whole()] * (chips + 1),
        out_specs=[whole()] * 2,
        out_shape=[six_shape] * 2,
        compiler_params=params(LIMITS["states"]),
        cost_estimate=cost(20 * keep.size, 20 * keep.size),
        name="states",
    )(from_chip, to_core, keep, other, *arrived)
    recv = lax.ppermute(theirs, "yz", swap_cores)
    recv, gains = lax.optimization_barrier((recv, gains.reshape(5, rows, lanes)))
    end_fwd, end_bwd = gains[3], gains[4]
    gains = gains[:3]
    others = [
        lax.ppermute(gains, "gx", [(at, (at + hop) % sections) for at in range(sections)])
        for hop in range(1, sections)
    ]
    arrivals = jnp.stack([gains] + others)
    every = jnp.stack([
        lax.dynamic_index_in_dim(arrivals, (section - at) % sections, 0, False)
        for at in range(sections)
    ])
    gain_f, gain_b, gain_c = every[:, 0], every[:, 1], every[:, 2]
    turned = [None] * sections
    turned[sections - 1] = jnp.zeros_like(gain_f[0])
    for at in range(sections - 2, -1, -1):
        turned[at] = gain_c[at + 1] + gain_b[at + 1] * gain_f[at + 1] * turned[at + 1]
    own = lambda value: lax.dynamic_index_in_dim(value, section, 0, False)
    turn = own(jnp.stack(turned))
    turn_out = own(gain_b) * turn
    start_gain, hop_fwd, hop_bwd = [], [], []
    one, zero = jnp.ones_like(gain_f[0]), jnp.zeros_like(gain_f[0])
    for to in range(sections):
        value = one
        for at in range(to):
            value = value * gain_f[at]
        start_gain.append(value)
        fwd_row, bwd_row = [], []
        for hop in range(1, sections):
            source = (to - hop) % sections
            value = one
            for at in range(min(source, to) + 1, max(source, to)):
                value = value * (gain_f if source < to else gain_b)[at]
            fwd_row.append(value if source < to else zero)
            bwd_row.append(value if source > to else zero)
        hop_fwd.append(jnp.stack(fwd_row))
        hop_bwd.append(jnp.stack(bwd_row))
    entering = own(jnp.stack(start_gain))[None] * widen(inflow)
    hop_fwd, hop_bwd = own(jnp.stack(hop_fwd)), own(jnp.stack(hop_bwd))
    own_gain = own(gain_f)

    tile = 8
    line_block = pl.BlockSpec((lines, tile, cells), lambda i: (0, i, 0))
    rate_tile = pl.BlockSpec((rows, tile, cells), lambda i: (0, i, 0))
    end_block = pl.BlockSpec((lines, lanes), lambda i: (0, 0))
    end_shape = jax.ShapeDtypeStruct((lines, lanes), F32)
    as_lines = lambda value: value.reshape(lines, span, cells)
    as_states = lambda value: value.reshape(6, n_fields, half, cells)
    swept, last, first = pl.pallas_call(
        functools.partial(sweep_kernel, rows),
        grid=(span // tile,),
        in_specs=[whole()] * 6 + [line_block] * 2 + [rate_tile] * 4,
        out_specs=[line_block, end_block, end_block],
        out_shape=[jax.ShapeDtypeStruct((lines, span, cells), F32), end_shape, end_shape],
        scratch_shapes=[
            pltpu.VMEM((n_us * span, cells), F32), pltpu.VMEM((n_ws * span, cells), F32)],
        compiler_params=params(LIMITS["sweep"]),
        cost_estimate=cost(2 * 3000 * fields.size, 12 * fields.size),
        name="sweep",
    )(smooth_mat, mixed_mat, wall_mat, sums, as_states(mine), as_states(recv),
      as_lines(smooth), as_lines(mixed), *rate_parts)
    last = last.reshape(n_fields, rows, lanes) * end_fwd[None]
    first = first.reshape(n_fields, rows, lanes) * end_bwd[None]

    upstream = first + turn_out[None] * last
    back = jnp.zeros_like(last)
    for hop in range(1, sections):
        payload = jnp.where(section + hop < sections, last, upstream)
        got = lax.ppermute(payload, "gx", [(at, (at + hop) % sections) for at in range(sections)])
        entering = entering + hop_fwd[hop - 1][None] * got
        back = back + hop_bwd[hop - 1][None] * got
    back = back + turn[None] * (own_gain[None] * entering + last)

    n_close = 8
    close_block = pl.BlockSpec((n_fields, n_close, span, cells), lambda i: (0, i, 0, 0))
    gain_block = pl.BlockSpec((n_close, span, cells), lambda i: (i, 0, 0))
    state_block = pl.BlockSpec((n_fields, n_close, lanes), lambda i: (0, i, 0))
    return pl.pallas_call(
        close_kernel,
        grid=(rows // n_close,),
        in_specs=[gain_block, gain_block, state_block, state_block, close_block],
        out_specs=close_block,
        out_shape=field_shape,
        compiler_params=params(LIMITS["close"]),
        cost_estimate=cost(4 * fields.size, 10 * fields.size),
        name="close",
    )(carry, tail, entering, back, swept.reshape(fields.shape))


def solution(mesh):
    placed = (
        P(None, "yz", None, "gx"), P(None, "yz", None), P("yz", None, "gx"), P("yz", None, "gx"),
        P(), P(), P(),
    )
    return jax.shard_map(
        shards, mesh=mesh, in_specs=placed, out_specs=P(None, "yz", None, "gx"), check_vma=False
    )
```

```python
import functools

import jax
import jax.numpy as jnp
import numpy as np
from jax import lax
from jax.experimental import pallas as pl
from jax.experimental.pallas import tpu as pltpu
from jax.sharding import PartitionSpec as P

F32, BF16 = jnp.float32, jnp.bfloat16
STEP = 0.5
LIMITS = {"mats": 56, "taps": 56, "chip": 8, "span": 24, "rates": 24, "states": 10, "sweep": 56, "close": 56}


def tridiagonal(points, below, centre, above, periodic):
    band = centre * np.eye(points) + below * np.eye(points, k=-1) + above * np.eye(points, k=1)
    if periodic:
        band[0, -1] += below
        band[-1, 0] += above
    return band


def operators(points, periodic):
    deriv = np.linalg.solve(
        tridiagonal(points, 0.25, 1.0, 0.25, periodic),
        tridiagonal(points, -0.75, 0.0, 0.75, periodic),
    )
    smooth = np.linalg.solve(
        tridiagonal(points, 0.499, 1.0, 0.499, periodic),
        tridiagonal(points, 0.4995, 0.999, 0.4995, periodic),
    )
    return smooth, deriv @ smooth, deriv @ deriv @ smooth


def wall_tables(points, devs):
    ops = operators(points, False)
    rows = points // devs

    def frame(first):
        vecs = np.stack(first)
        basis = []
        for vec in vecs:
            for _ in range(3):
                for other in basis:
                    vec = vec - other * (other @ vec)
            basis.append(vec / np.linalg.norm(vec))
        return np.stack(basis)

    above, below = {}, {}
    for edge in range(rows, points, rows):
        above[edge] = np.zeros((3, points))
        above[edge][:, edge:] = frame([op[edge - 1, edge:] for op in ops])
        below[edge] = np.zeros((3, points))
        below[edge][:, :edge] = frame([op[edge, :edge] for op in ops])
    nothing = np.zeros((3, points))
    above_at = lambda edge: above.get(edge, nothing)
    below_at = lambda edge: below.get(edge, nothing)

    def carry_above(target, source):
        return above_at(target) @ above_at(source).T

    def carry_below(target, source):
        return below_at(target) @ below_at(source).T

    chips = devs // 2
    taps = np.zeros((devs, 6, rows))
    local = np.zeros((devs, 3, rows, rows))
    reach = np.zeros((devs, 3, rows, 6))
    chip_mix = np.zeros((devs, 2, 3, 6))
    from_chip = np.zeros((devs, 2, max(chips - 1, 1), 3, 3))
    to_core = np.zeros((devs, 4, 3, 3))
    eye = np.eye(3)
    for dev in range(devs):
        low, high = dev * rows, (dev + 1) * rows
        own = slice(low, high)
        taps[dev, :3] = above_at(low)[:, own]
        taps[dev, 3:] = below_at(high)[:, own]
        for at, op in enumerate(ops):
            local[dev, at] = op[own, own]
            reach[dev, at, :, :3] = op[own] @ above_at(high).T
            reach[dev, at, :, 3:] = op[own] @ below_at(low).T
        chip, core = divmod(dev, 2)
        start, middle, end = 2 * chip * rows, (2 * chip + 1) * rows, (2 * chip + 2) * rows
        up = [eye, carry_above(start, middle)]
        down = [carry_below(end, middle), eye]
        chip_mix[dev, 0] = np.concatenate([up[core], up[1 - core]], 1)
        chip_mix[dev, 1] = np.concatenate([down[core], down[1 - core]], 1)
        for at in range(1, chips):
            other = chip ^ at
            if other > chip:
                from_chip[dev, 0, at - 1] = carry_above(end, 2 * other * rows)
            else:
                from_chip[dev, 1, at - 1] = carry_below(start, (2 * other + 2) * rows)
        above_core = [carry_above(middle, end), eye]
        below_core = [eye, carry_below(middle, start)]
        to_core[dev, 0], to_core[dev, 1] = above_core[core], above_core[1 - core]
        to_core[dev, 2], to_core[dev, 3] = below_core[core], below_core[1 - core]
    return taps, local, reach, chip_mix, from_chip, to_core


def wall_layout(local, reach, fields):
    devs, _, rows, _ = local.shape
    states = reach.transpose(0, 1, 3, 2)
    us = -(-6 * fields // 32) * 32
    ws = -(-(2 * fields * rows + us + 2 * fields) // 128) * 128 - 2 * fields * rows - us
    width = 2 * fields * rows + us + ws
    owner = np.full(width, -1)
    parts = np.zeros((devs, 3, rows, width))
    for field in range(fields):
        at = slice(field * rows, (field + 1) * rows)
        owner[at] = field
        parts[:, 1:, :, at] = local[:, 1:]
        at = slice(fields * rows + us + field * rows, fields * rows + us + (field + 1) * rows)
        owner[at] = field
        parts[:, 0, :, at] = local[:, 0]
        for k in range(6):
            at = fields * rows + k * fields + field
            owner[at] = field
            parts[:, 1:, :, at] = states[:, 1:, k]
        for place, k in enumerate((0, 3)):
            at = 2 * fields * rows + us + place * fields + field
            owner[at] = field
            parts[:, 0, :, at] = states[:, 0, k]
    pick = (owner[None] == np.arange(fields)[:, None]).astype(np.float64)
    tall = np.concatenate([parts] * fields, axis=2)
    same = np.repeat(pick, rows, axis=0)
    tall[:, 2] *= same
    tall[:, 0] *= same
    return tall[:, [1, 2, 0]], pick, us, ws


def split(value):
    high = np.asarray(value, np.float32).astype(BF16)
    low = (np.asarray(value, np.float32) - high.astype(np.float32)).astype(BF16)
    return np.concatenate([high, high, low], axis=-1)


def parted(value):
    high = value.astype(BF16)
    return high, (value - high.astype(F32)).astype(BF16)


def dot(a, b):
    return jnp.dot(a, b, preferred_element_type=F32)


def stacked(value):
    high, low = parted(value)
    return jnp.concatenate([high, low, high], axis=0)


def padded(value, to):
    if value.shape[0] == to:
        return value
    return jnp.concatenate([value, jnp.zeros((to - value.shape[0], value.shape[1]), F32)], axis=0)


def running(value, twice):
    high, low = parted(value)
    return dot(jnp.concatenate([high, low], axis=1), twice)


def mats_kernel(dev_ref, flux_wall_ref, flux_span_ref, visc_ref, wall_rows_ref, wall_cols_ref,
                wall_ref, span_rows_ref, span_cols_ref, span_ref, wall_out, span_out):
    exact = functools.partial(jnp.dot, precision=lax.Precision.HIGHEST, preferred_element_type=F32)
    for flux_ref, rows_ref, cols_ref, ops, out in (
        (flux_wall_ref, wall_rows_ref, wall_cols_ref, wall_ref[0], wall_out),
        (flux_span_ref, span_rows_ref, span_cols_ref, span_ref[...], span_out),
    ):
        cols = cols_ref[...]
        by_field = exact(-STEP * flux_ref[...], cols)
        parts = []
        for _ in range(3):
            part = by_field.astype(BF16)
            by_field = by_field - part.astype(F32)
            parts.append(part.astype(F32))
        mixing = dot(rows_ref[...], jnp.concatenate(parts, axis=0).astype(BF16))
        visc = exact(STEP * visc_ref[...], cols)[0:1]
        high, low = parted(mixing * ops[0] + visc * ops[1] + ops[2])
        width = cols.shape[1]
        out[:, :width] = high
        out[:, width : 2 * width] = high
        out[:, 2 * width :] = low


def taps_kernel(taps_ref, x_ref, keep_ref, send_ref):
    rows = x_ref.shape[1]
    me = lax.axis_index("yz")
    base = me * (6 * rows)
    half = x_ref.shape[2] // 2
    step = half if half <= 48 else 8
    core = me % 2
    for out_ref, offset in ((keep_ref, core * half), (send_ref, (1 - core) * half)):

        def piece(at, _):
            source = pl.multiple_of(offset + at * step, 8)
            sums = [None] * 6
            for row in range(rows):
                value = x_ref[0, row, pl.ds(source, step), :]
                for tap in range(6):
                    term = taps_ref[base + (tap * rows + row)] * value
                    sums[tap] = term if row == 0 else sums[tap] + term
            for tap in range(6):
                out_ref[tap, 0, pl.ds(pl.multiple_of(at * step, 8), step), :] = sums[tap]
            return 0

        lax.fori_loop(0, half // step, piece, 0)


def chip_kernel(chips, mix_ref, own_ref, other_ref, *out_refs):
    me = lax.axis_index("yz")
    chip, base = me // 2, me * 36
    lines = own_ref.shape[1]

    def piece(at, _):
        span = pl.ds(pl.multiple_of(at * 24, 8), 24)
        sums = []
        for side in range(2):
            terms = [own_ref[3 * side + k, span, :] for k in range(3)]
            terms += [other_ref[3 * side + k, span, :] for k in range(3)]
            sums.append(
                [sum(mix_ref[base + (18 * side + 6 * row + k)] * terms[k] for k in range(6)) for row in range(3)]
            )
        for at_chip in range(1, chips):
            lower = chip < (chip ^ at_chip)
            for row in range(3):
                out_refs[at_chip - 1][row, span, :] = jnp.where(lower, sums[1][row], sums[0][row])
        return 0

    lax.fori_loop(0, lines // 24, piece, 0)


def states_kernel(chips, from_ref, to_ref, own_ref, other_ref, *refs):
    me = lax.axis_index("yz")
    core, from_base, to_base = me % 2, me * (18 * (chips - 1)), me * 36
    arrived, (mine_ref, theirs_ref) = refs[: chips - 1], refs[chips - 1 :]
    lines = own_ref.shape[1]

    def piece(at, _):
        span = pl.ds(pl.multiple_of(at * 24, 8), 24)
        for side in range(2):
            into = [jnp.zeros((24, own_ref.shape[2]), F32) for _ in range(3)]
            for at_chip in range(chips - 1):
                for k in range(3):
                    value = arrived[at_chip][k, span, :]
                    for row in range(3):
                        into[row] += from_ref[from_base + (9 * (side * (chips - 1) + at_chip) + 3 * row + k)] * value
            for_mine = (core == 0) if side == 0 else (core == 1)
            for row in range(3):
                to_mine = sum(to_ref[to_base + (18 * side + 3 * row + k)] * into[k] for k in range(3))
                to_theirs = sum(to_ref[to_base + (18 * side + 9 + 3 * row + k)] * into[k] for k in range(3))
                near = 3 * side + row
                mine_ref[near, span, :] = to_mine + jnp.where(for_mine, other_ref[near, span, :], 0.0)
                theirs_ref[near, span, :] = to_theirs + jnp.where(
                    for_mine, 0.0, own_ref[near, span, :]
                )
        return 0

    lax.fori_loop(0, lines // 24, piece, 0)


def span_kernel(smooth_ref, mixed_ref, x_ref, smooth_out, mixed_out):
    fields, pair, span, cells = x_ref.shape
    wide = jnp.concatenate([x_ref[:, row].reshape(fields * span, cells) for row in range(pair)], 1)
    mixed = dot(mixed_ref[...], stacked(padded(wide, mixed_ref.shape[1] // 3)))
    for field in range(fields):
        part = slice(field * span, (field + 1) * span)
        smooth = dot(smooth_ref[...], stacked(wide[part]))
        for row in range(pair):
            place = slice(row * cells, (row + 1) * cells)
            smooth_out[field, row] = smooth[:, place]
            mixed_out[field, row] = mixed[part, place]


def rates_kernel(last_ref, logs_ref, sums_ref, ends_ref, fwd_ref, bwd_ref, *outs):
    win_ref, rf_ref, wout_ref, rb_ref, carry_ref, tail_ref, gains_ref = outs
    rows, span, cells = fwd_ref.shape

    def gathered(rate, mat):
        value = jnp.log(rate)
        high = value.astype(BF16)
        rest = value - high.astype(F32)
        middle = rest.astype(BF16)
        low = (rest - middle.astype(F32)).astype(BF16)
        terms = jnp.concatenate([high, middle, low], axis=1)
        both = dot(terms, mat)
        return both[:, :cells], both[:, cells:], terms

    def across(which, terms):
        mat = ends_ref[which][:, : terms.shape[1]]
        return [lax.dot_general(mat, terms[row * span : (row + 1) * span], (((1,), (1,)), ((), ())),
                                preferred_element_type=F32) for row in range(rows)]

    fwd = fwd_ref[...].reshape(rows * span, cells)
    bwd = bwd_ref[...].reshape(rows * span, cells)
    lane = lax.broadcasted_iota(jnp.int32, fwd.shape, 1)
    relative, absolute, terms = gathered(fwd, logs_ref[0])
    fwd_ends = across(0, terms)
    win_ref[...] = ((1.0 - fwd) * jnp.exp(-relative)).reshape(rows, span, cells)
    rf_ref[...] = jnp.exp(relative).reshape(rows, span, cells)
    entered = jnp.exp(absolute)
    relative, absolute, terms = gathered(bwd, logs_ref[1])
    bwd_ends = across(1, terms)
    grow = jnp.exp(relative)
    keep = jnp.where((lane == cells - 1) & (last_ref[0] == 1), 1.0, 1.0 - bwd)
    weight = keep * jnp.exp(-relative)
    wout_ref[...] = weight.reshape(rows, span, cells)
    rb_ref[...] = grow.reshape(rows, span, cells)
    tail_ref[...] = jnp.exp(absolute).reshape(rows, span, cells)
    high, low = parted(entered * weight)
    terms = jnp.concatenate([high, low], axis=1)
    carry_ref[...] = (grow * dot(terms, sums_ref[...])).reshape(rows, span, cells)
    carry_ends = across(2, terms)
    gains_ref[...] = jnp.zeros_like(gains_ref)
    for row in range(rows):
        ends_f, ends_b = jnp.exp(fwd_ends[row]), jnp.exp(bwd_ends[row])
        gains = (ends_f[0:1], ends_b[0:1], carry_ends[row][0:1] * ends_b[1:2], ends_f[1:2],
                 ends_b[1:2])
        for at, gain in enumerate(gains):
            gains_ref[at, row, :, :span] = gain


def sweep_kernel(rows, smooth_ref, mixed_ref, wall_ref, sums_ref, mine_ref,
                 recv_ref, u_ref, w_ref, win_ref, rf_ref, wout_ref, rb_ref, out_ref, last_ref,
                 first_ref, us_ref, ws_ref):
    tile = u_ref.shape[1]
    cells = u_ref.shape[2]
    fields, half = mine_ref.shape[1], mine_ref.shape[2]
    span = 2 * half
    lines = fields * rows
    at = pl.program_id(0)

    @pl.when(at == 0)
    def _():
        us_ref[pl.ds(6 * fields * span, us_ref.shape[0] - 6 * fields * span), :] = jnp.zeros(
            (us_ref.shape[0] - 6 * fields * span, cells), F32)
        ws_ref[pl.ds(2 * fields * span, ws_ref.shape[0] - 2 * fields * span), :] = jnp.zeros(
            (ws_ref.shape[0] - 2 * fields * span, cells), F32)
        last_ref[...] = jnp.zeros_like(last_ref)
        first_ref[...] = jnp.zeros_like(first_ref)
        first_core = lax.axis_index("yz") % 2 == 0

        def state(k):
            mine, recv = mine_ref[k], recv_ref[k]
            both = [jnp.where(first_core, mine, recv), jnp.where(first_core, recv, mine)]
            return jnp.concatenate(both, axis=1).reshape(fields * span, cells)

        for pair in ((0, 3), (1, 2), (4, 5)):
            wide = jnp.concatenate([state(k) for k in pair], axis=1)
            for field in range(fields):
                part = slice(field * span, (field + 1) * span)
                smooth = dot(smooth_ref[...], stacked(wide[part]))
                for place, k in enumerate(pair):
                    us_ref[pl.ds((k * fields + field) * span, span), :] = smooth[
                        :, place * cells : (place + 1) * cells
                    ]
            if pair == (0, 3):
                mixed = dot(mixed_ref[...], stacked(padded(wide, mixed_ref.shape[1] // 3)))
                for place in range(2):
                    ws_ref[pl.ds(place * fields * span, fields * span), :] = mixed[
                        :, place * cells : (place + 1) * cells
                    ]

    u_flat = u_ref.reshape(lines * tile, cells)
    w_flat = w_ref.reshape(lines * tile, cells)
    out_flat = out_ref.reshape(lines * tile, cells)
    rate_flat = [ref.reshape(rows * tile, cells) for ref in (win_ref, rf_ref, wout_ref, rb_ref)]
    lane = lax.broadcasted_iota(jnp.int32, (lines, last_ref.shape[1]), 1)
    last, first = last_ref[...], first_ref[...]
    rates = [
        jnp.concatenate([
            value for z in range(tile) for value in [ref[pl.ds(z, rows, stride=tile), :]] * fields], 0)
        for ref in rate_flat
    ]
    rights = []
    for z in range(0, tile, 2):
        wide = []
        for zz in (z, z + 1):
            where = at * tile + zz
            wide.append(jnp.concatenate([
                u_flat[pl.ds(zz, lines, stride=tile), :],
                us_ref[pl.ds(where, us_ref.shape[0] // span, stride=span), :],
                w_flat[pl.ds(zz, lines, stride=tile), :],
                ws_ref[pl.ds(where, ws_ref.shape[0] // span, stride=span), :]], 0))
        right = dot(wall_ref[...], stacked(jnp.concatenate(wide, 1)))
        rights += [right[:, :cells], right[:, cells:]]
    ahead = running(jnp.concatenate(rights, 0) * rates[0], sums_ref[0])
    ahead, total = ahead[:, :cells] * rates[1], ahead[:, cells:]
    result = running(ahead * rates[2], sums_ref[1])
    result, total_back = result[:, :cells] * rates[3], result[:, cells:]
    for z in range(tile):
        part = slice(z * lines, (z + 1) * lines)
        here = lane == at * tile + z
        out_flat[pl.ds(z, lines, stride=tile), :] = result[part]
        last = jnp.where(here, total[part], last)
        first = jnp.where(here, total_back[part], first)
    last_ref[...] = last
    first_ref[...] = first


def close_kernel(carry_ref, tail_ref, enter_ref, back_ref, t_ref, out_ref):
    fields, rows, span, _ = t_ref.shape
    for field in range(fields):
        enter = enter_ref[field].T[:span]
        back = back_ref[field].T[:span]
        for row in range(rows):
            out_ref[field, row] = (
                t_ref[field, row]
                + carry_ref[row] * enter[:, row : row + 1]
                + tail_ref[row] * back[:, row : row + 1]
            )


def params(limit):
    return pltpu.CompilerParams(vmem_limit_bytes=limit * 2**20)


def cost(flops, moved):
    return pl.CostEstimate(flops=int(flops), bytes_accessed=int(moved), transcendentals=0)


def whole(memory=pltpu.VMEM):
    return pl.BlockSpec(memory_space=memory)


SMEM = whole(pltpu.SMEM)


def shards(fields, inflow, rates_fwd, rates_bwd, flux_wall, flux_span, viscosity):
    n_fields, rows, span, cells = fields.shape
    devs, sections = lax.axis_size("yz"), lax.axis_size("gx")
    me, section = lax.axis_index("yz"), lax.axis_index("gx")
    chips, half = devs // 2, span // 2
    lines = n_fields * rows
    taps, local, reach, *maps = wall_tables(rows * devs, devs)
    flat = lambda table: jnp.asarray(np.asarray(table, np.float32).reshape(-1))
    taps, chip_mix, from_chip, to_core = (flat(table) for table in (taps, *maps))
    f32 = lambda table: jnp.asarray(np.asarray(table, np.float32))
    span_ops = operators(span, True)
    wall_ops, wall_pick, n_us, n_ws = wall_layout(local, reach, n_fields)
    width = wall_pick.shape[1]
    span_width = -(-n_fields * span // 128) * 128
    pad = lambda mat: np.pad(mat, [(0, 0)] * (mat.ndim - 1) + [(0, span_width - n_fields * span)])
    size = 8
    up_to = lambda mat: np.pad(mat, ((0, size - n_fields), (0, 0)))
    pick_rows = lambda count: jnp.asarray(np.tile(
        np.pad(np.repeat(np.eye(n_fields), count, axis=0), ((0, 0), (0, size - n_fields))), (1, 3)
    ).astype(BF16))
    span_cols = pad(np.repeat(np.eye(n_fields), span, axis=1))
    tiny = jnp.zeros((3 * size, size), F32)
    tiny = lax.dynamic_update_slice(tiny, flux_wall, (0, 0))
    tiny = lax.dynamic_update_slice(tiny, flux_span, (size, 0))
    tiny = lax.dynamic_update_slice(tiny, viscosity[None], (2 * size, 0))
    smooth_mat = jnp.asarray(split(span_ops[0]))
    dev_block = lambda *shape: pl.BlockSpec(
        (1, *shape), lambda i, dev: (dev[0],) + (0,) * len(shape))
    full_block = lambda *shape: pl.BlockSpec(shape, lambda i, dev: (0,) * len(shape))
    all_span = n_fields * span
    wall_mat, mixed_mat = pl.pallas_call(
        mats_kernel,
        grid_spec=pltpu.PrefetchScalarGridSpec(
            num_scalar_prefetch=1,
            grid=(1,),
            in_specs=[
                pl.BlockSpec((size, size), lambda i, dev: (0, 0)),
                pl.BlockSpec((size, size), lambda i, dev: (1, 0)),
                pl.BlockSpec((size, size), lambda i, dev: (2, 0)),
                full_block(lines, 3 * size), full_block(size, width), dev_block(3, lines, width),
                full_block(all_span, 3 * size), full_block(size, span_width),
                full_block(3, all_span, span_width)],
            out_specs=[full_block(lines, 3 * width), full_block(all_span, 3 * span_width)],
        ),
        out_shape=[
            jax.ShapeDtypeStruct((lines, 3 * width), BF16),
            jax.ShapeDtypeStruct((all_span, 3 * span_width), BF16)],
        compiler_params=params(LIMITS["mats"]),
        cost_estimate=cost(10**7, 8 * 10**6),
        name="mats",
    )(me.astype(jnp.int32).reshape(1), tiny, tiny, tiny, pick_rows(rows), f32(up_to(wall_pick)),
      f32(wall_ops), pick_rows(span), f32(up_to(span_cols)),
      f32(np.stack([
          pad(np.tile(span_ops[1], (n_fields, n_fields))),
          pad(np.kron(np.eye(n_fields), span_ops[2])),
          pad(np.kron(np.eye(n_fields), span_ops[0]))])))
    tri = np.triu(np.ones((cells, cells), np.float32))
    ones = np.ones_like(tri)
    twice = lambda mat: np.concatenate([mat, mat], 0)
    sums = jnp.asarray(np.stack([
        twice(np.concatenate([tri, ones], 1)), twice(np.concatenate([tri.T, ones], 1))
    ])).astype(BF16)
    logs_fwd = tri - tri[:, cells // 2 - 1 :][:, :1]
    logs_bwd = tri.T - tri.T[:, cells // 2 :][:, :1]
    thrice = lambda mat: np.concatenate([mat, mat, mat], 0)
    logs = jnp.asarray(np.stack([
        thrice(np.concatenate([logs_fwd, tri], 1)), thrice(np.concatenate([logs_bwd, tri.T], 1))
    ])).astype(BF16)

    tap_shape = jax.ShapeDtypeStruct((6, n_fields, half, cells), F32)
    tap_block = pl.BlockSpec((6, 1, half, cells), lambda f: (0, f, 0, 0))
    keep, send = pl.pallas_call(
        taps_kernel,
        grid=(n_fields,),
        in_specs=[SMEM, pl.BlockSpec((1, rows, span, cells), lambda f: (f, 0, 0, 0))],
        out_specs=[tap_block, tap_block],
        out_shape=[tap_shape, tap_shape],
        compiler_params=params(LIMITS["taps"]),
        cost_estimate=cost(12 * fields.size, 4 * fields.size),
        name="taps",
    )(taps, fields)
    swap_cores = [(dev, dev ^ 1) for dev in range(devs)]
    tap_lines = n_fields * half
    keep = keep.reshape(6, tap_lines, cells)
    other = lax.ppermute(send.reshape(6, tap_lines, cells), "yz", swap_cores)
    part_shape = jax.ShapeDtypeStruct((3, tap_lines, cells), F32)
    outgoing = pl.pallas_call(
        functools.partial(chip_kernel, chips),
        in_specs=[SMEM, whole(), whole()],
        out_specs=[whole()] * (chips - 1),
        out_shape=[part_shape] * (chips - 1),
        compiler_params=params(LIMITS["chip"]),
        cost_estimate=cost(6 * keep.size, 12 * keep.size),
        name="chip",
    )(chip_mix, keep, other)
    held_fields, held_fwd, held_bwd, wall_mat, mixed_mat, *outgoing = lax.optimization_barrier(
        (fields, rates_fwd, rates_bwd, wall_mat, mixed_mat, *outgoing))
    arrived = [
        lax.ppermute(value, "yz", [(dev, dev ^ (2 * (at + 1))) for dev in range(devs)])
        for at, value in enumerate(outgoing)
    ]
    n_span = 4
    pair_block = pl.BlockSpec((n_fields, n_span, span, cells), lambda i: (0, i, 0, 0))
    field_shape = jax.ShapeDtypeStruct(fields.shape, F32)
    smooth, mixed = pl.pallas_call(
        span_kernel,
        grid=(rows // n_span,),
        in_specs=[whole(), whole(), pair_block],
        out_specs=[pair_block, pair_block],
        out_shape=[pltpu.HBM(fields.shape, F32)] * 2,
        compiler_params=params(LIMITS["span"]),
        cost_estimate=cost(2 * 4000 * fields.size, 12 * fields.size),
        name="span",
    )(smooth_mat, mixed_mat, held_fields)

    n_rate = 8
    rate_block = pl.BlockSpec((n_rate, span, cells), lambda i: (i, 0, 0))
    rate_shape = jax.ShapeDtypeStruct(rates_fwd.shape, F32)
    is_last = (section == sections - 1).astype(jnp.int32).reshape(1)
    lanes = -(-span // 128) * 128
    widen = lambda value: jnp.pad(value, [(0, 0)] * (value.ndim - 1) + [(0, lanes - span)])
    ends = np.zeros((3, 16, 3 * cells))
    ends[:, 0] = 1.0
    ends[0, 1] = np.tile(np.arange(cells) >= cells // 2, 3)
    ends[1, 1] = np.tile(np.arange(cells) < cells // 2, 3)
    *rate_parts, carry, tail, gains = pl.pallas_call(
        rates_kernel,
        grid=(rows // n_rate,),
        in_specs=[SMEM, whole(), whole(), whole(), rate_block, rate_block],
        out_specs=[rate_block] * 6 + [pl.BlockSpec((5, n_rate, 1, lanes), lambda i: (0, i, 0, 0))],
        out_shape=[pltpu.HBM(rates_fwd.shape, F32)] * 6 + [jax.ShapeDtypeStruct((5, rows, 1, lanes), F32)],
        compiler_params=params(LIMITS["rates"]),
        cost_estimate=cost(2 * 4000 * rates_fwd.size, 32 * rates_fwd.size),
        name="rates",
    )(is_last, logs, sums[1, :, :cells], jnp.asarray(ends.astype(BF16)), held_fwd, held_bwd)
    smooth, mixed, gains, *arrived = lax.optimization_barrier((smooth, mixed, gains, *arrived))
    six_shape = jax.ShapeDtypeStruct((6, tap_lines, cells), F32)
    mine, theirs = pl.pallas_call(
        functools.partial(states_kernel, chips),
        in_specs=[SMEM] * 2 + [whole()] * (chips + 1),
        out_specs=[whole()] * 2,
        out_shape=[six_shape] * 2,
        compiler_params=params(LIMITS["states"]),
        cost_estimate=cost(20 * keep.size, 20 * keep.size),
        name="states",
    )(from_chip, to_core, keep, other, *arrived)
    recv = lax.ppermute(theirs, "yz", swap_cores)
    recv, gains = lax.optimization_barrier((recv, gains.reshape(5, rows, lanes)))
    end_fwd, end_bwd = gains[3], gains[4]
    gains = gains[:3]
    others = [
        lax.ppermute(gains, "gx", [(at, at ^ hop) for at in range(sections)])
        for hop in range(1, sections)
    ]
    arrivals = jnp.stack([gains] + others)
    every = jnp.stack([
        lax.dynamic_index_in_dim(arrivals, section ^ at, 0, False)
        for at in range(sections)
    ])
    gain_f, gain_b, gain_c = every[:, 0], every[:, 1], every[:, 2]
    turned = [None] * sections
    turned[sections - 1] = jnp.zeros_like(gain_f[0])
    for at in range(sections - 2, -1, -1):
        turned[at] = gain_c[at + 1] + gain_b[at + 1] * gain_f[at + 1] * turned[at + 1]
    own = lambda value: lax.dynamic_index_in_dim(value, section, 0, False)
    turn = own(jnp.stack(turned))
    turn_out = own(gain_b) * turn
    start_gain, hop_fwd, hop_bwd = [], [], []
    one, zero = jnp.ones_like(gain_f[0]), jnp.zeros_like(gain_f[0])
    for to in range(sections):
        value = one
        for at in range(to):
            value = value * gain_f[at]
        start_gain.append(value)
        fwd_row, bwd_row = [], []
        for hop in range(1, sections):
            source = to ^ hop
            value = one
            for at in range(min(source, to) + 1, max(source, to)):
                value = value * (gain_f if source < to else gain_b)[at]
            fwd_row.append(value if source < to else zero)
            bwd_row.append(value if source > to else zero)
        hop_fwd.append(jnp.stack(fwd_row))
        hop_bwd.append(jnp.stack(bwd_row))
    entering = own(jnp.stack(start_gain))[None] * widen(inflow)
    hop_fwd, hop_bwd = own(jnp.stack(hop_fwd)), own(jnp.stack(hop_bwd))
    own_gain = own(gain_f)

    tile = 8
    line_block = pl.BlockSpec((lines, tile, cells), lambda i: (0, i, 0))
    rate_tile = pl.BlockSpec((rows, tile, cells), lambda i: (0, i, 0))
    end_block = pl.BlockSpec((lines, lanes), lambda i: (0, 0))
    end_shape = jax.ShapeDtypeStruct((lines, lanes), F32)
    as_lines = lambda value: value.reshape(lines, span, cells)
    as_states = lambda value: value.reshape(6, n_fields, half, cells)
    swept, last, first = pl.pallas_call(
        functools.partial(sweep_kernel, rows),
        grid=(span // tile,),
        in_specs=[whole()] * 6 + [line_block] * 2 + [rate_tile] * 4,
        out_specs=[line_block, end_block, end_block],
        out_shape=[jax.ShapeDtypeStruct((lines, span, cells), F32), end_shape, end_shape],
        scratch_shapes=[
            pltpu.VMEM((n_us * span, cells), F32), pltpu.VMEM((n_ws * span, cells), F32)],
        compiler_params=params(LIMITS["sweep"]),
        cost_estimate=cost(2 * 3000 * fields.size, 12 * fields.size),
        name="sweep",
    )(smooth_mat, mixed_mat, wall_mat, sums, as_states(mine), as_states(recv),
      as_lines(smooth), as_lines(mixed), *rate_parts)
    last = last.reshape(n_fields, rows, lanes) * end_fwd[None]
    first = first.reshape(n_fields, rows, lanes) * end_bwd[None]

    upstream = first + turn_out[None] * last
    back = jnp.zeros_like(last)
    for hop in range(1, sections):
        payload = jnp.where((section ^ hop) > section, last, upstream)
        got = lax.ppermute(payload, "gx", [(at, at ^ hop) for at in range(sections)])
        entering = entering + hop_fwd[hop - 1][None] * got
        back = back + hop_bwd[hop - 1][None] * got
    back = back + turn[None] * (own_gain[None] * entering + last)

    n_close = 8
    close_block = pl.BlockSpec((n_fields, n_close, span, cells), lambda i: (0, i, 0, 0))
    gain_block = pl.BlockSpec((n_close, span, cells), lambda i: (i, 0, 0))
    state_block = pl.BlockSpec((n_fields, n_close, lanes), lambda i: (0, i, 0))
    return pl.pallas_call(
        close_kernel,
        grid=(rows // n_close,),
        in_specs=[gain_block, gain_block, state_block, state_block, close_block],
        out_specs=close_block,
        out_shape=field_shape,
        compiler_params=params(LIMITS["close"]),
        cost_estimate=cost(4 * fields.size, 10 * fields.size),
        name="close",
    )(carry, tail, entering, back, swept.reshape(fields.shape))


def solution(mesh):
    placed = (
        P(None, "yz", None, "gx"), P(None, "yz", None), P("yz", None, "gx"), P("yz", None, "gx"),
        P(), P(), P(),
    )
    return jax.shard_map(
        shards, mesh=mesh, in_specs=placed, out_specs=P(None, "yz", None, "gx"), check_vma=False
    )
```

```python
import functools

import jax
import jax.numpy as jnp
import numpy as np
from jax import lax
from jax.experimental import pallas as pl
from jax.experimental.pallas import tpu as pltpu
from jax.sharding import PartitionSpec as P

F32, BF16 = jnp.float32, jnp.bfloat16
STEP = 0.5
LIMITS = {"mats": 56, "taps": 56, "chip": 8, "span": 24, "rates": 24, "states": 10, "sweep": 52, "close": 16}


def tridiagonal(points, below, centre, above, periodic):
    band = centre * np.eye(points) + below * np.eye(points, k=-1) + above * np.eye(points, k=1)
    if periodic:
        band[0, -1] += below
        band[-1, 0] += above
    return band


def operators(points, periodic):
    deriv = np.linalg.solve(
        tridiagonal(points, 0.25, 1.0, 0.25, periodic),
        tridiagonal(points, -0.75, 0.0, 0.75, periodic),
    )
    smooth = np.linalg.solve(
        tridiagonal(points, 0.499, 1.0, 0.499, periodic),
        tridiagonal(points, 0.4995, 0.999, 0.4995, periodic),
    )
    return smooth, deriv @ smooth, deriv @ deriv @ smooth


def wall_tables(points, devs):
    ops = operators(points, False)
    rows = points // devs

    def frame(first):
        vecs = np.stack(first)
        basis = []
        for vec in vecs:
            for _ in range(3):
                for other in basis:
                    vec = vec - other * (other @ vec)
            basis.append(vec / np.linalg.norm(vec))
        return np.stack(basis)

    above, below = {}, {}
    for edge in range(rows, points, rows):
        above[edge] = np.zeros((3, points))
        above[edge][:, edge:] = frame([op[edge - 1, edge:] for op in ops])
        below[edge] = np.zeros((3, points))
        below[edge][:, :edge] = frame([op[edge, :edge] for op in ops])
    nothing = np.zeros((3, points))
    above_at = lambda edge: above.get(edge, nothing)
    below_at = lambda edge: below.get(edge, nothing)

    def carry_above(target, source):
        return above_at(target) @ above_at(source).T

    def carry_below(target, source):
        return below_at(target) @ below_at(source).T

    chips = devs // 2
    taps = np.zeros((devs, 6, rows))
    local = np.zeros((devs, 3, rows, rows))
    reach = np.zeros((devs, 3, rows, 6))
    chip_mix = np.zeros((devs, 2, 3, 6))
    from_chip = np.zeros((devs, 2, max(chips - 1, 1), 3, 3))
    to_core = np.zeros((devs, 4, 3, 3))
    eye = np.eye(3)
    for dev in range(devs):
        low, high = dev * rows, (dev + 1) * rows
        own = slice(low, high)
        taps[dev, :3] = above_at(low)[:, own]
        taps[dev, 3:] = below_at(high)[:, own]
        for at, op in enumerate(ops):
            local[dev, at] = op[own, own]
            reach[dev, at, :, :3] = op[own] @ above_at(high).T
            reach[dev, at, :, 3:] = op[own] @ below_at(low).T
        chip, core = divmod(dev, 2)
        start, middle, end = 2 * chip * rows, (2 * chip + 1) * rows, (2 * chip + 2) * rows
        up = [eye, carry_above(start, middle)]
        down = [carry_below(end, middle), eye]
        chip_mix[dev, 0] = np.concatenate([up[core], up[1 - core]], 1)
        chip_mix[dev, 1] = np.concatenate([down[core], down[1 - core]], 1)
        for at in range(1, chips):
            other = chip ^ at
            if other > chip:
                from_chip[dev, 0, at - 1] = carry_above(end, 2 * other * rows)
            else:
                from_chip[dev, 1, at - 1] = carry_below(start, (2 * other + 2) * rows)
        above_core = [carry_above(middle, end), eye]
        below_core = [eye, carry_below(middle, start)]
        to_core[dev, 0], to_core[dev, 1] = above_core[core], above_core[1 - core]
        to_core[dev, 2], to_core[dev, 3] = below_core[core], below_core[1 - core]
    return taps, local, reach, chip_mix, from_chip, to_core


def wall_layout(local, reach, fields):
    devs, _, rows, _ = local.shape
    states = reach.transpose(0, 1, 3, 2)
    us = -(-6 * fields // 32) * 32
    ws = -(-(2 * fields * rows + us + 2 * fields) // 128) * 128 - 2 * fields * rows - us
    width = 2 * fields * rows + us + ws
    owner = np.full(width, -1)
    parts = np.zeros((devs, 3, rows, width))
    for field in range(fields):
        at = slice(field * rows, (field + 1) * rows)
        owner[at] = field
        parts[:, 1:, :, at] = local[:, 1:]
        at = slice(fields * rows + us + field * rows, fields * rows + us + (field + 1) * rows)
        owner[at] = field
        parts[:, 0, :, at] = local[:, 0]
        for k in range(6):
            at = fields * rows + k * fields + field
            owner[at] = field
            parts[:, 1:, :, at] = states[:, 1:, k]
        for place, k in enumerate((0, 3)):
            at = 2 * fields * rows + us + place * fields + field
            owner[at] = field
            parts[:, 0, :, at] = states[:, 0, k]
    pick = (owner[None] == np.arange(fields)[:, None]).astype(np.float64)
    tall = np.concatenate([parts] * fields, axis=2)
    same = np.repeat(pick, rows, axis=0)
    tall[:, 2] *= same
    tall[:, 0] *= same
    return tall[:, [1, 2, 0]], pick, us, ws


def split(value):
    high = np.asarray(value, np.float32).astype(BF16)
    low = (np.asarray(value, np.float32) - high.astype(np.float32)).astype(BF16)
    return np.concatenate([high, high, low], axis=-1)


def parted(value):
    high = value.astype(BF16)
    return high, (value - high.astype(F32)).astype(BF16)


def dot(a, b):
    return jnp.dot(a, b, preferred_element_type=F32)


def stacked(value):
    high, low = parted(value)
    return jnp.concatenate([high, low, high], axis=0)


def padded(value, to):
    if value.shape[0] == to:
        return value
    return jnp.concatenate([value, jnp.zeros((to - value.shape[0], value.shape[1]), F32)], axis=0)


def running(value, twice):
    high, low = parted(value)
    return dot(jnp.concatenate([high, low], axis=1), twice)


def mats_kernel(dev_ref, flux_wall_ref, flux_span_ref, visc_ref, wall_rows_ref, wall_cols_ref,
                wall_ref, span_rows_ref, span_cols_ref, span_ref, wall_out, span_out):
    exact = functools.partial(jnp.dot, precision=lax.Precision.HIGHEST, preferred_element_type=F32)
    for flux_ref, rows_ref, cols_ref, ops, out in (
        (flux_wall_ref, wall_rows_ref, wall_cols_ref, wall_ref[0], wall_out),
        (flux_span_ref, span_rows_ref, span_cols_ref, span_ref[...], span_out),
    ):
        cols = cols_ref[...]
        by_field = exact(-STEP * flux_ref[...], cols)
        parts = []
        for _ in range(3):
            part = by_field.astype(BF16)
            by_field = by_field - part.astype(F32)
            parts.append(part.astype(F32))
        mixing = dot(rows_ref[...], jnp.concatenate(parts, axis=0).astype(BF16))
        visc = exact(STEP * visc_ref[...], cols)[0:1]
        high, low = parted(mixing * ops[0] + visc * ops[1] + ops[2])
        width = cols.shape[1]
        out[:, :width] = high
        out[:, width : 2 * width] = high
        out[:, 2 * width :] = low


def taps_kernel(taps_ref, x_ref, keep_ref, send_ref):
    rows = x_ref.shape[1]
    me = lax.axis_index("yz")
    base = me * (6 * rows)
    half = x_ref.shape[2] // 2
    step = half if half <= 48 else 8
    core = me % 2
    for out_ref, offset in ((keep_ref, core * half), (send_ref, (1 - core) * half)):

        def piece(at, _):
            source = pl.multiple_of(offset + at * step, 8)
            sums = [None] * 6
            for row in range(rows):
                value = x_ref[0, row, pl.ds(source, step), :]
                for tap in range(6):
                    term = taps_ref[base + (tap * rows + row)] * value
                    sums[tap] = term if row == 0 else sums[tap] + term
            for tap in range(6):
                out_ref[tap, 0, pl.ds(pl.multiple_of(at * step, 8), step), :] = sums[tap]
            return 0

        lax.fori_loop(0, half // step, piece, 0)


def chip_kernel(chips, mix_ref, own_ref, other_ref, *out_refs):
    me = lax.axis_index("yz")
    chip, base = me // 2, me * 36
    lines = own_ref.shape[1]

    def piece(at, _):
        span = pl.ds(pl.multiple_of(at * 24, 8), 24)
        sums = []
        for side in range(2):
            terms = [own_ref[3 * side + k, span, :] for k in range(3)]
            terms += [other_ref[3 * side + k, span, :] for k in range(3)]
            sums.append(
                [sum(mix_ref[base + (18 * side + 6 * row + k)] * terms[k] for k in range(6)) for row in range(3)]
            )
        for at_chip in range(1, chips):
            lower = chip < (chip ^ at_chip)
            for row in range(3):
                out_refs[at_chip - 1][row, span, :] = jnp.where(lower, sums[1][row], sums[0][row])
        return 0

    lax.fori_loop(0, lines // 24, piece, 0)


def states_kernel(chips, from_ref, to_ref, own_ref, other_ref, *refs):
    me = lax.axis_index("yz")
    core, from_base, to_base = me % 2, me * (18 * (chips - 1)), me * 36
    arrived, (mine_ref, theirs_ref) = refs[: chips - 1], refs[chips - 1 :]
    lines = own_ref.shape[1]

    def piece(at, _):
        span = pl.ds(pl.multiple_of(at * 24, 8), 24)
        for side in range(2):
            into = [jnp.zeros((24, own_ref.shape[2]), F32) for _ in range(3)]
            for at_chip in range(chips - 1):
                for k in range(3):
                    value = arrived[at_chip][k, span, :]
                    for row in range(3):
                        into[row] += from_ref[from_base + (9 * (side * (chips - 1) + at_chip) + 3 * row + k)] * value
            for_mine = (core == 0) if side == 0 else (core == 1)
            for row in range(3):
                to_mine = sum(to_ref[to_base + (18 * side + 3 * row + k)] * into[k] for k in range(3))
                to_theirs = sum(to_ref[to_base + (18 * side + 9 + 3 * row + k)] * into[k] for k in range(3))
                near = 3 * side + row
                mine_ref[near, span, :] = to_mine + jnp.where(for_mine, other_ref[near, span, :], 0.0)
                theirs_ref[near, span, :] = to_theirs + jnp.where(
                    for_mine, 0.0, own_ref[near, span, :]
                )
        return 0

    lax.fori_loop(0, lines // 24, piece, 0)


def span_kernel(smooth_ref, mixed_ref, x_ref, smooth_out, mixed_out):
    fields, pair, span, cells = x_ref.shape
    wide = jnp.concatenate([x_ref[:, row].reshape(fields * span, cells) for row in range(pair)], 1)
    mixed = dot(mixed_ref[...], stacked(padded(wide, mixed_ref.shape[1] // 3)))
    for field in range(fields):
        part = slice(field * span, (field + 1) * span)
        smooth = dot(smooth_ref[...], stacked(wide[part]))
        for row in range(pair):
            place = slice(row * cells, (row + 1) * cells)
            smooth_out[field, row] = smooth[:, place]
            mixed_out[field, row] = mixed[part, place]


def rates_kernel(last_ref, logs_ref, sums_ref, ends_ref, fwd_ref, bwd_ref, *outs):
    win_ref, rf_ref, wout_ref, rb_ref, carry_ref, tail_ref, gains_ref = outs
    rows, span, cells = fwd_ref.shape

    def gathered(rate, mat):
        value = jnp.log(rate)
        high = value.astype(BF16)
        rest = value - high.astype(F32)
        middle = rest.astype(BF16)
        low = (rest - middle.astype(F32)).astype(BF16)
        terms = jnp.concatenate([high, middle, low], axis=1)
        both = dot(terms, mat)
        return both[:, :cells], both[:, cells:], terms

    def across(which, terms):
        mat = ends_ref[which][:, : terms.shape[1]]
        return [lax.dot_general(mat, terms[row * span : (row + 1) * span], (((1,), (1,)), ((), ())),
                                preferred_element_type=F32) for row in range(rows)]

    fwd = fwd_ref[...].reshape(rows * span, cells)
    bwd = bwd_ref[...].reshape(rows * span, cells)
    lane = lax.broadcasted_iota(jnp.int32, fwd.shape, 1)
    relative, absolute, terms = gathered(fwd, logs_ref[0])
    fwd_ends = across(0, terms)
    win_ref[...] = ((1.0 - fwd) * jnp.exp(-relative)).reshape(rows, span, cells)
    rf_ref[...] = jnp.exp(relative).reshape(rows, span, cells)
    entered = jnp.exp(absolute)
    relative, absolute, terms = gathered(bwd, logs_ref[1])
    bwd_ends = across(1, terms)
    grow = jnp.exp(relative)
    keep = jnp.where((lane == cells - 1) & (last_ref[0] == 1), 1.0, 1.0 - bwd)
    weight = keep * jnp.exp(-relative)
    wout_ref[...] = weight.reshape(rows, span, cells)
    rb_ref[...] = grow.reshape(rows, span, cells)
    tail_ref[...] = jnp.exp(absolute).reshape(rows, span, cells)
    high, low = parted(entered * weight)
    terms = jnp.concatenate([high, low], axis=1)
    carry_ref[...] = (grow * dot(terms, sums_ref[...])).reshape(rows, span, cells)
    carry_ends = across(2, terms)
    gains_ref[...] = jnp.zeros_like(gains_ref)
    for row in range(rows):
        ends_f, ends_b = jnp.exp(fwd_ends[row]), jnp.exp(bwd_ends[row])
        gains = (ends_f[0:1], ends_b[0:1], carry_ends[row][0:1] * ends_b[1:2], ends_f[1:2],
                 ends_b[1:2])
        for at, gain in enumerate(gains):
            gains_ref[at, row, :, :span] = gain


def sweep_kernel(rows, smooth_ref, mixed_ref, wall_ref, sums_ref, mine_ref,
                 recv_ref, u_ref, w_ref, win_ref, rf_ref, wout_ref, rb_ref, out_ref, last_ref,
                 first_ref, us_ref, ws_ref):
    tile = u_ref.shape[1]
    cells = u_ref.shape[2]
    fields, half = mine_ref.shape[1], mine_ref.shape[2]
    span = 2 * half
    lines = fields * rows
    at = pl.program_id(0)

    @pl.when(at == 0)
    def _():
        us_ref[pl.ds(6 * fields * span, us_ref.shape[0] - 6 * fields * span), :] = jnp.zeros(
            (us_ref.shape[0] - 6 * fields * span, cells), F32)
        ws_ref[pl.ds(2 * fields * span, ws_ref.shape[0] - 2 * fields * span), :] = jnp.zeros(
            (ws_ref.shape[0] - 2 * fields * span, cells), F32)
        last_ref[...] = jnp.zeros_like(last_ref)
        first_ref[...] = jnp.zeros_like(first_ref)
        first_core = lax.axis_index("yz") % 2 == 0

        def state(k):
            mine, recv = mine_ref[k], recv_ref[k]
            both = [jnp.where(first_core, mine, recv), jnp.where(first_core, recv, mine)]
            return jnp.concatenate(both, axis=1).reshape(fields * span, cells)

        for pair in ((0, 3), (1, 2), (4, 5)):
            wide = jnp.concatenate([state(k) for k in pair], axis=1)
            for field in range(fields):
                part = slice(field * span, (field + 1) * span)
                smooth = dot(smooth_ref[...], stacked(wide[part]))
                for place, k in enumerate(pair):
                    us_ref[pl.ds((k * fields + field) * span, span), :] = smooth[
                        :, place * cells : (place + 1) * cells
                    ]
            if pair == (0, 3):
                mixed = dot(mixed_ref[...], stacked(padded(wide, mixed_ref.shape[1] // 3)))
                for place in range(2):
                    ws_ref[pl.ds(place * fields * span, fields * span), :] = mixed[
                        :, place * cells : (place + 1) * cells
                    ]

    u_flat = u_ref.reshape(lines * tile, cells)
    w_flat = w_ref.reshape(lines * tile, cells)
    out_flat = out_ref.reshape(lines * tile, cells)
    rate_flat = [ref.reshape(rows * tile, cells) for ref in (win_ref, rf_ref, wout_ref, rb_ref)]
    lane = lax.broadcasted_iota(jnp.int32, (lines, last_ref.shape[1]), 1)
    last, first = last_ref[...], first_ref[...]
    rates = [
        jnp.concatenate([
            value for z in range(tile) for value in [ref[pl.ds(z, rows, stride=tile), :]] * fields], 0)
        for ref in rate_flat
    ]
    rights = []
    for z in range(0, tile, 2):
        wide = []
        for zz in (z, z + 1):
            where = at * tile + zz
            wide.append(jnp.concatenate([
                u_flat[pl.ds(zz, lines, stride=tile), :],
                us_ref[pl.ds(where, us_ref.shape[0] // span, stride=span), :],
                w_flat[pl.ds(zz, lines, stride=tile), :],
                ws_ref[pl.ds(where, ws_ref.shape[0] // span, stride=span), :]], 0))
        right = dot(wall_ref[...], stacked(jnp.concatenate(wide, 1)))
        rights += [right[:, :cells], right[:, cells:]]
    ahead = running(jnp.concatenate(rights, 0) * rates[0], sums_ref[0])
    ahead, total = ahead[:, :cells] * rates[1], ahead[:, cells:]
    result = running(ahead * rates[2], sums_ref[1])
    result, total_back = result[:, :cells] * rates[3], result[:, cells:]
    for z in range(tile):
        part = slice(z * lines, (z + 1) * lines)
        here = lane == at * tile + z
        out_flat[pl.ds(z, lines, stride=tile), :] = result[part]
        last = jnp.where(here, total[part], last)
        first = jnp.where(here, total_back[part], first)
    last_ref[...] = last
    first_ref[...] = first


def close_kernel(carry_ref, tail_ref, enter_ref, back_ref, t_ref, out_ref):
    fields, rows, span, _ = t_ref.shape
    for field in range(fields):
        enter = enter_ref[field].T[:span]
        back = back_ref[field].T[:span]
        for row in range(rows):
            out_ref[field, row] = (
                t_ref[field, row]
                + carry_ref[row] * enter[:, row : row + 1]
                + tail_ref[row] * back[:, row : row + 1]
            )


def params(limit):
    return pltpu.CompilerParams(vmem_limit_bytes=limit * 2**20)


def cost(flops, moved):
    return pl.CostEstimate(flops=int(flops), bytes_accessed=int(moved), transcendentals=0)


def whole(memory=pltpu.VMEM):
    return pl.BlockSpec(memory_space=memory)


SMEM = whole(pltpu.SMEM)


def shards(fields, inflow, rates_fwd, rates_bwd, flux_wall, flux_span, viscosity):
    n_fields, rows, span, cells = fields.shape
    devs, sections = lax.axis_size("yz"), lax.axis_size("gx")
    me, section = lax.axis_index("yz"), lax.axis_index("gx")
    chips, half = devs // 2, span // 2
    lines = n_fields * rows
    taps, local, reach, *maps = wall_tables(rows * devs, devs)
    flat = lambda table: jnp.asarray(np.asarray(table, np.float32).reshape(-1))
    taps, chip_mix, from_chip, to_core = (flat(table) for table in (taps, *maps))
    f32 = lambda table: jnp.asarray(np.asarray(table, np.float32))
    span_ops = operators(span, True)
    wall_ops, wall_pick, n_us, n_ws = wall_layout(local, reach, n_fields)
    width = wall_pick.shape[1]
    span_width = -(-n_fields * span // 128) * 128
    pad = lambda mat: np.pad(mat, [(0, 0)] * (mat.ndim - 1) + [(0, span_width - n_fields * span)])
    size = 8
    up_to = lambda mat: np.pad(mat, ((0, size - n_fields), (0, 0)))
    pick_rows = lambda count: jnp.asarray(np.tile(
        np.pad(np.repeat(np.eye(n_fields), count, axis=0), ((0, 0), (0, size - n_fields))), (1, 3)
    ).astype(BF16))
    span_cols = pad(np.repeat(np.eye(n_fields), span, axis=1))
    tiny = jnp.zeros((3 * size, size), F32)
    tiny = lax.dynamic_update_slice(tiny, flux_wall, (0, 0))
    tiny = lax.dynamic_update_slice(tiny, flux_span, (size, 0))
    tiny = lax.dynamic_update_slice(tiny, viscosity[None], (2 * size, 0))
    smooth_mat = jnp.asarray(split(span_ops[0]))
    dev_block = lambda *shape: pl.BlockSpec(
        (1, *shape), lambda i, dev: (dev[0],) + (0,) * len(shape))
    full_block = lambda *shape: pl.BlockSpec(shape, lambda i, dev: (0,) * len(shape))
    all_span = n_fields * span
    wall_mat, mixed_mat = pl.pallas_call(
        mats_kernel,
        grid_spec=pltpu.PrefetchScalarGridSpec(
            num_scalar_prefetch=1,
            grid=(1,),
            in_specs=[
                pl.BlockSpec((size, size), lambda i, dev: (0, 0)),
                pl.BlockSpec((size, size), lambda i, dev: (1, 0)),
                pl.BlockSpec((size, size), lambda i, dev: (2, 0)),
                full_block(lines, 3 * size), full_block(size, width), dev_block(3, lines, width),
                full_block(all_span, 3 * size), full_block(size, span_width),
                full_block(3, all_span, span_width)],
            out_specs=[full_block(lines, 3 * width), full_block(all_span, 3 * span_width)],
        ),
        out_shape=[
            jax.ShapeDtypeStruct((lines, 3 * width), BF16),
            jax.ShapeDtypeStruct((all_span, 3 * span_width), BF16)],
        compiler_params=params(LIMITS["mats"]),
        cost_estimate=cost(10**7, 8 * 10**6),
        name="mats",
    )(me.astype(jnp.int32).reshape(1), tiny, tiny, tiny, pick_rows(rows), f32(up_to(wall_pick)),
      f32(wall_ops), pick_rows(span), f32(up_to(span_cols)),
      f32(np.stack([
          pad(np.tile(span_ops[1], (n_fields, n_fields))),
          pad(np.kron(np.eye(n_fields), span_ops[2])),
          pad(np.kron(np.eye(n_fields), span_ops[0]))])))
    tri = np.triu(np.ones((cells, cells), np.float32))
    ones = np.ones_like(tri)
    twice = lambda mat: np.concatenate([mat, mat], 0)
    sums = jnp.asarray(np.stack([
        twice(np.concatenate([tri, ones], 1)), twice(np.concatenate([tri.T, ones], 1))
    ])).astype(BF16)
    logs_fwd = tri - tri[:, cells // 2 - 1 :][:, :1]
    logs_bwd = tri.T - tri.T[:, cells // 2 :][:, :1]
    thrice = lambda mat: np.concatenate([mat, mat, mat], 0)
    logs = jnp.asarray(np.stack([
        thrice(np.concatenate([logs_fwd, tri], 1)), thrice(np.concatenate([logs_bwd, tri.T], 1))
    ])).astype(BF16)

    tap_shape = jax.ShapeDtypeStruct((6, n_fields, half, cells), F32)
    tap_block = pl.BlockSpec((6, 1, half, cells), lambda f: (0, f, 0, 0))
    keep, send = pl.pallas_call(
        taps_kernel,
        grid=(n_fields,),
        in_specs=[SMEM, pl.BlockSpec((1, rows, span, cells), lambda f: (f, 0, 0, 0))],
        out_specs=[tap_block, tap_block],
        out_shape=[tap_shape, tap_shape],
        compiler_params=params(LIMITS["taps"]),
        cost_estimate=cost(12 * fields.size, 4 * fields.size),
        name="taps",
    )(taps, fields)
    swap_cores = [(dev, dev ^ 1) for dev in range(devs)]
    tap_lines = n_fields * half
    keep = keep.reshape(6, tap_lines, cells)
    other = lax.ppermute(send.reshape(6, tap_lines, cells), "yz", swap_cores)
    part_shape = jax.ShapeDtypeStruct((3, tap_lines, cells), F32)
    outgoing = pl.pallas_call(
        functools.partial(chip_kernel, chips),
        in_specs=[SMEM, whole(), whole()],
        out_specs=[whole()] * (chips - 1),
        out_shape=[part_shape] * (chips - 1),
        compiler_params=params(LIMITS["chip"]),
        cost_estimate=cost(6 * keep.size, 12 * keep.size),
        name="chip",
    )(chip_mix, keep, other)
    held_fields, held_fwd, held_bwd, wall_mat, mixed_mat, *outgoing = lax.optimization_barrier(
        (fields, rates_fwd, rates_bwd, wall_mat, mixed_mat, *outgoing))
    arrived = [
        lax.ppermute(value, "yz", [(dev, dev ^ (2 * (at + 1))) for dev in range(devs)])
        for at, value in enumerate(outgoing)
    ]
    n_span = 4
    pair_block = pl.BlockSpec((n_fields, n_span, span, cells), lambda i: (0, i, 0, 0))
    field_shape = jax.ShapeDtypeStruct(fields.shape, F32)
    smooth, mixed = pl.pallas_call(
        span_kernel,
        grid=(rows // n_span,),
        in_specs=[whole(), whole(), pair_block],
        out_specs=[pair_block, pair_block],
        out_shape=[pltpu.HBM(fields.shape, F32)] * 2,
        compiler_params=params(LIMITS["span"]),
        cost_estimate=cost(2 * 4000 * fields.size, 12 * fields.size),
        name="span",
    )(smooth_mat, mixed_mat, held_fields)

    n_rate = 8
    rate_block = pl.BlockSpec((n_rate, span, cells), lambda i: (i, 0, 0))
    rate_shape = jax.ShapeDtypeStruct(rates_fwd.shape, F32)
    is_last = (section == sections - 1).astype(jnp.int32).reshape(1)
    lanes = -(-span // 128) * 128
    widen = lambda value: jnp.pad(value, [(0, 0)] * (value.ndim - 1) + [(0, lanes - span)])
    ends = np.zeros((3, 16, 3 * cells))
    ends[:, 0] = 1.0
    ends[0, 1] = np.tile(np.arange(cells) >= cells // 2, 3)
    ends[1, 1] = np.tile(np.arange(cells) < cells // 2, 3)
    *rate_parts, carry, tail, gains = pl.pallas_call(
        rates_kernel,
        grid=(rows // n_rate,),
        in_specs=[SMEM, whole(), whole(), whole(), rate_block, rate_block],
        out_specs=[rate_block] * 6 + [pl.BlockSpec((5, n_rate, 1, lanes), lambda i: (0, i, 0, 0))],
        out_shape=[pltpu.HBM(rates_fwd.shape, F32)] * 6 + [jax.ShapeDtypeStruct((5, rows, 1, lanes), F32)],
        compiler_params=params(LIMITS["rates"]),
        cost_estimate=cost(2 * 4000 * rates_fwd.size, 32 * rates_fwd.size),
        name="rates",
    )(is_last, logs, sums[1, :, :cells], jnp.asarray(ends.astype(BF16)), held_fwd, held_bwd)
    smooth, mixed, gains, *arrived = lax.optimization_barrier((smooth, mixed, gains, *arrived))
    six_shape = jax.ShapeDtypeStruct((6, tap_lines, cells), F32)
    mine, theirs = pl.pallas_call(
        functools.partial(states_kernel, chips),
        in_specs=[SMEM] * 2 + [whole()] * (chips + 1),
        out_specs=[whole()] * 2,
        out_shape=[six_shape] * 2,
        compiler_params=params(LIMITS["states"]),
        cost_estimate=cost(20 * keep.size, 20 * keep.size),
        name="states",
    )(from_chip, to_core, keep, other, *arrived)
    recv = lax.ppermute(theirs, "yz", swap_cores)
    recv, gains = lax.optimization_barrier((recv, gains.reshape(5, rows, lanes)))
    end_fwd, end_bwd = gains[3], gains[4]
    gains = gains[:3]
    others = [
        lax.ppermute(gains, "gx", [(at, at ^ hop) for at in range(sections)])
        for hop in range(1, sections)
    ]
    arrivals = jnp.stack([gains] + others)
    every = jnp.stack([
        lax.dynamic_index_in_dim(arrivals, section ^ at, 0, False)
        for at in range(sections)
    ])
    gain_f, gain_b, gain_c = every[:, 0], every[:, 1], every[:, 2]
    turned = [None] * sections
    turned[sections - 1] = jnp.zeros_like(gain_f[0])
    for at in range(sections - 2, -1, -1):
        turned[at] = gain_c[at + 1] + gain_b[at + 1] * gain_f[at + 1] * turned[at + 1]
    own = lambda value: lax.dynamic_index_in_dim(value, section, 0, False)
    turn = own(jnp.stack(turned))
    turn_out = own(gain_b) * turn
    start_gain, hop_fwd, hop_bwd = [], [], []
    one, zero = jnp.ones_like(gain_f[0]), jnp.zeros_like(gain_f[0])
    for to in range(sections):
        value = one
        for at in range(to):
            value = value * gain_f[at]
        start_gain.append(value)
        fwd_row, bwd_row = [], []
        for hop in range(1, sections):
            source = to ^ hop
            value = one
            for at in range(min(source, to) + 1, max(source, to)):
                value = value * (gain_f if source < to else gain_b)[at]
            fwd_row.append(value if source < to else zero)
            bwd_row.append(value if source > to else zero)
        hop_fwd.append(jnp.stack(fwd_row))
        hop_bwd.append(jnp.stack(bwd_row))
    entering = own(jnp.stack(start_gain))[None] * widen(inflow)
    hop_fwd, hop_bwd = own(jnp.stack(hop_fwd)), own(jnp.stack(hop_bwd))
    own_gain = own(gain_f)

    tile = 8
    line_block = pl.BlockSpec((lines, tile, cells), lambda i: (0, i, 0))
    rate_tile = pl.BlockSpec((rows, tile, cells), lambda i: (0, i, 0))
    end_block = pl.BlockSpec((lines, lanes), lambda i: (0, 0))
    end_shape = jax.ShapeDtypeStruct((lines, lanes), F32)
    as_lines = lambda value: value.reshape(lines, span, cells)
    as_states = lambda value: value.reshape(6, n_fields, half, cells)
    swept, last, first = pl.pallas_call(
        functools.partial(sweep_kernel, rows),
        grid=(span // tile,),
        in_specs=[whole()] * 6 + [line_block] * 2 + [rate_tile] * 4,
        out_specs=[line_block, end_block, end_block],
        out_shape=[pltpu.VMEM((lines, span, cells), F32), end_shape, end_shape],
        scratch_shapes=[
            pltpu.VMEM((n_us * span, cells), F32), pltpu.VMEM((n_ws * span, cells), F32)],
        compiler_params=params(LIMITS["sweep"]),
        cost_estimate=cost(2 * 3000 * fields.size, 12 * fields.size),
        name="sweep",
    )(smooth_mat, mixed_mat, wall_mat, sums, as_states(mine), as_states(recv),
      as_lines(smooth), as_lines(mixed), *rate_parts)
    last = last.reshape(n_fields, rows, lanes) * end_fwd[None]
    first = first.reshape(n_fields, rows, lanes) * end_bwd[None]

    upstream = first + turn_out[None] * last
    back = jnp.zeros_like(last)
    for hop in range(1, sections):
        payload = jnp.where((section ^ hop) > section, last, upstream)
        got = lax.ppermute(payload, "gx", [(at, at ^ hop) for at in range(sections)])
        entering = entering + hop_fwd[hop - 1][None] * got
        back = back + hop_bwd[hop - 1][None] * got
    back = back + turn[None] * (own_gain[None] * entering + last)

    n_close = 8
    close_block = pl.BlockSpec((n_fields, n_close, span, cells), lambda i: (0, i, 0, 0))
    gain_block = pl.BlockSpec((n_close, span, cells), lambda i: (i, 0, 0))
    state_block = pl.BlockSpec((n_fields, n_close, lanes), lambda i: (0, i, 0))
    return pl.pallas_call(
        close_kernel,
        grid=(rows // n_close,),
        in_specs=[gain_block, gain_block, state_block, state_block, close_block],
        out_specs=close_block,
        out_shape=field_shape,
        compiler_params=params(LIMITS["close"]),
        cost_estimate=cost(4 * fields.size, 10 * fields.size),
        name="close",
    )(carry, tail, entering, back, swept.reshape(fields.shape))


def solution(mesh):
    placed = (
        P(None, "yz", None, "gx"), P(None, "yz", None), P("yz", None, "gx"), P("yz", None, "gx"),
        P(), P(), P(),
    )
    return jax.shard_map(
        shards, mesh=mesh, in_specs=placed, out_specs=P(None, "yz", None, "gx"), check_vma=False
    )
```

```python
import functools

import jax
import jax.numpy as jnp
import numpy as np
from jax import lax
from jax.experimental import pallas as pl
from jax.experimental.pallas import tpu as pltpu
from jax.sharding import PartitionSpec as P

F32, BF16 = jnp.float32, jnp.bfloat16
STEP = 0.5
LIMITS = {"mats": 56, "taps": 56, "chip": 8, "span": 24, "rates": 24, "states": 10, "sweep": 52, "close": 16}


def tridiagonal(points, below, centre, above, periodic):
    band = centre * np.eye(points) + below * np.eye(points, k=-1) + above * np.eye(points, k=1)
    if periodic:
        band[0, -1] += below
        band[-1, 0] += above
    return band


def operators(points, periodic):
    deriv = np.linalg.solve(
        tridiagonal(points, 0.25, 1.0, 0.25, periodic),
        tridiagonal(points, -0.75, 0.0, 0.75, periodic),
    )
    smooth = np.linalg.solve(
        tridiagonal(points, 0.499, 1.0, 0.499, periodic),
        tridiagonal(points, 0.4995, 0.999, 0.4995, periodic),
    )
    return smooth, deriv @ smooth, deriv @ deriv @ smooth


def wall_tables(points, devs):
    ops = operators(points, False)
    rows = points // devs

    def frame(first):
        vecs = np.stack(first)
        basis = []
        for vec in vecs:
            for _ in range(3):
                for other in basis:
                    vec = vec - other * (other @ vec)
            basis.append(vec / np.linalg.norm(vec))
        return np.stack(basis)

    above, below = {}, {}
    for edge in range(rows, points, rows):
        above[edge] = np.zeros((3, points))
        above[edge][:, edge:] = frame([op[edge - 1, edge:] for op in ops])
        below[edge] = np.zeros((3, points))
        below[edge][:, :edge] = frame([op[edge, :edge] for op in ops])
    nothing = np.zeros((3, points))
    above_at = lambda edge: above.get(edge, nothing)
    below_at = lambda edge: below.get(edge, nothing)

    def carry_above(target, source):
        return above_at(target) @ above_at(source).T

    def carry_below(target, source):
        return below_at(target) @ below_at(source).T

    chips = devs // 2
    taps = np.zeros((devs, 6, rows))
    local = np.zeros((devs, 3, rows, rows))
    reach = np.zeros((devs, 3, rows, 6))
    chip_mix = np.zeros((devs, 2, 3, 6))
    from_chip = np.zeros((devs, 2, max(chips - 1, 1), 3, 3))
    to_core = np.zeros((devs, 4, 3, 3))
    eye = np.eye(3)
    for dev in range(devs):
        low, high = dev * rows, (dev + 1) * rows
        own = slice(low, high)
        taps[dev, :3] = above_at(low)[:, own]
        taps[dev, 3:] = below_at(high)[:, own]
        for at, op in enumerate(ops):
            local[dev, at] = op[own, own]
            reach[dev, at, :, :3] = op[own] @ above_at(high).T
            reach[dev, at, :, 3:] = op[own] @ below_at(low).T
        chip, core = divmod(dev, 2)
        start, middle, end = 2 * chip * rows, (2 * chip + 1) * rows, (2 * chip + 2) * rows
        up = [eye, carry_above(start, middle)]
        down = [carry_below(end, middle), eye]
        chip_mix[dev, 0] = np.concatenate([up[core], up[1 - core]], 1)
        chip_mix[dev, 1] = np.concatenate([down[core], down[1 - core]], 1)
        for at in range(1, chips):
            other = chip ^ at
            if other > chip:
                from_chip[dev, 0, at - 1] = carry_above(end, 2 * other * rows)
            else:
                from_chip[dev, 1, at - 1] = carry_below(start, (2 * other + 2) * rows)
        above_core = [carry_above(middle, end), eye]
        below_core = [eye, carry_below(middle, start)]
        to_core[dev, 0], to_core[dev, 1] = above_core[core], above_core[1 - core]
        to_core[dev, 2], to_core[dev, 3] = below_core[core], below_core[1 - core]
    return taps, local, reach, chip_mix, from_chip, to_core


def wall_layout(local, reach, fields):
    devs, _, rows, _ = local.shape
    states = reach.transpose(0, 1, 3, 2)
    us = -(-6 * fields // 32) * 32
    ws = -(-(2 * fields * rows + us + 2 * fields) // 128) * 128 - 2 * fields * rows - us
    width = 2 * fields * rows + us + ws
    owner = np.full(width, -1)
    parts = np.zeros((devs, 3, rows, width))
    for field in range(fields):
        at = slice(field * rows, (field + 1) * rows)
        owner[at] = field
        parts[:, 1:, :, at] = local[:, 1:]
        at = slice(fields * rows + us + field * rows, fields * rows + us + (field + 1) * rows)
        owner[at] = field
        parts[:, 0, :, at] = local[:, 0]
        for k in range(6):
            at = fields * rows + k * fields + field
            owner[at] = field
            parts[:, 1:, :, at] = states[:, 1:, k]
        for place, k in enumerate((0, 3)):
            at = 2 * fields * rows + us + place * fields + field
            owner[at] = field
            parts[:, 0, :, at] = states[:, 0, k]
    pick = (owner[None] == np.arange(fields)[:, None]).astype(np.float64)
    return parts[:, [1, 2, 0]], pick, us, ws


def split(value):
    high = np.asarray(value, np.float32).astype(BF16)
    low = (np.asarray(value, np.float32) - high.astype(np.float32)).astype(BF16)
    return np.concatenate([high, high, low], axis=-1)


def parted(value):
    high = value.astype(BF16)
    return high, (value - high.astype(F32)).astype(BF16)


def dot(a, b):
    return jnp.dot(a, b, preferred_element_type=F32)


def stacked(value):
    high, low = parted(value)
    return jnp.concatenate([high, low, high], axis=0)


def padded(value, to):
    if value.shape[0] == to:
        return value
    return jnp.concatenate([value, jnp.zeros((to - value.shape[0], value.shape[1]), F32)], axis=0)


def running(value, twice):
    high, low = parted(value)
    return dot(jnp.concatenate([high, low], axis=1), twice)


def mats_kernel(dev_ref, flux_wall_ref, flux_span_ref, visc_ref, wall_cols_ref, wall_ref,
                span_cols_ref, span_ref, wall_out, span_out):
    exact = functools.partial(jnp.dot, precision=lax.Precision.HIGHEST, preferred_element_type=F32)
    for flux_ref, cols_ref, ops, out in (
        (flux_wall_ref, wall_cols_ref, wall_ref[0], wall_out),
        (flux_span_ref, span_cols_ref, span_ref[...], span_out),
    ):
        cols = cols_ref[...]
        mixing = exact(-STEP * flux_ref[...], cols)
        own = exact(STEP * visc_ref[...], cols)[0:1] * ops[1] + ops[2]
        points, width = own.shape
        high, low = parted(jnp.concatenate([
            mixing[field : field + 1] * ops[0] + cols[field : field + 1] * own
            for field in range(out.shape[0] // points)], axis=0))
        out[:, :width] = high
        out[:, width : 2 * width] = high
        out[:, 2 * width :] = low


def taps_kernel(taps_ref, x_ref, keep_ref, send_ref):
    rows = x_ref.shape[1]
    me = lax.axis_index("yz")
    base = me * (6 * rows)
    half = x_ref.shape[2] // 2
    step = half if half <= 48 else 8
    core = me % 2
    for out_ref, offset in ((keep_ref, core * half), (send_ref, (1 - core) * half)):

        def piece(at, _):
            source = pl.multiple_of(offset + at * step, 8)
            sums = [None] * 6
            for row in range(rows):
                value = x_ref[0, row, pl.ds(source, step), :]
                for tap in range(6):
                    term = taps_ref[base + (tap * rows + row)] * value
                    sums[tap] = term if row == 0 else sums[tap] + term
            for tap in range(6):
                out_ref[tap, 0, pl.ds(pl.multiple_of(at * step, 8), step), :] = sums[tap]
            return 0

        lax.fori_loop(0, half // step, piece, 0)


def chip_kernel(chips, mix_ref, own_ref, other_ref, *out_refs):
    me = lax.axis_index("yz")
    chip, base = me // 2, me * 36
    lines = own_ref.shape[1]

    def piece(at, _):
        span = pl.ds(pl.multiple_of(at * 24, 8), 24)
        sums = []
        for side in range(2):
            terms = [own_ref[3 * side + k, span, :] for k in range(3)]
            terms += [other_ref[3 * side + k, span, :] for k in range(3)]
            sums.append(
                [sum(mix_ref[base + (18 * side + 6 * row + k)] * terms[k] for k in range(6)) for row in range(3)]
            )
        for at_chip in range(1, chips):
            lower = chip < (chip ^ at_chip)
            for row in range(3):
                out_refs[at_chip - 1][row, span, :] = jnp.where(lower, sums[1][row], sums[0][row])
        return 0

    lax.fori_loop(0, lines // 24, piece, 0)


def states_kernel(chips, from_ref, to_ref, own_ref, other_ref, *refs):
    me = lax.axis_index("yz")
    core, from_base, to_base = me % 2, me * (18 * (chips - 1)), me * 36
    arrived, (mine_ref, theirs_ref) = refs[: chips - 1], refs[chips - 1 :]
    lines = own_ref.shape[1]

    def piece(at, _):
        span = pl.ds(pl.multiple_of(at * 24, 8), 24)
        for side in range(2):
            into = [jnp.zeros((24, own_ref.shape[2]), F32) for _ in range(3)]
            for at_chip in range(chips - 1):
                for k in range(3):
                    value = arrived[at_chip][k, span, :]
                    for row in range(3):
                        into[row] += from_ref[from_base + (9 * (side * (chips - 1) + at_chip) + 3 * row + k)] * value
            for_mine = (core == 0) if side == 0 else (core == 1)
            for row in range(3):
                to_mine = sum(to_ref[to_base + (18 * side + 3 * row + k)] * into[k] for k in range(3))
                to_theirs = sum(to_ref[to_base + (18 * side + 9 + 3 * row + k)] * into[k] for k in range(3))
                near = 3 * side + row
                mine_ref[near, span, :] = to_mine + jnp.where(for_mine, other_ref[near, span, :], 0.0)
                theirs_ref[near, span, :] = to_theirs + jnp.where(
                    for_mine, 0.0, own_ref[near, span, :]
                )
        return 0

    lax.fori_loop(0, lines // 24, piece, 0)


def span_kernel(smooth_ref, mixed_ref, x_ref, smooth_out, mixed_out):
    fields, pair, span, cells = x_ref.shape
    wide = jnp.concatenate([x_ref[:, row].reshape(fields * span, cells) for row in range(pair)], 1)
    mixed = dot(mixed_ref[...], stacked(padded(wide, mixed_ref.shape[1] // 3)))
    for field in range(fields):
        part = slice(field * span, (field + 1) * span)
        smooth = dot(smooth_ref[...], stacked(wide[part]))
        for row in range(pair):
            place = slice(row * cells, (row + 1) * cells)
            smooth_out[field, row] = smooth[:, place]
            mixed_out[field, row] = mixed[part, place]


def rates_kernel(last_ref, logs_ref, sums_ref, ends_ref, fwd_ref, bwd_ref, *outs):
    win_ref, rf_ref, wout_ref, rb_ref, carry_ref, tail_ref, gains_ref = outs
    rows, span, cells = fwd_ref.shape

    def gathered(rate, mat):
        value = jnp.log(rate)
        high = value.astype(BF16)
        rest = value - high.astype(F32)
        middle = rest.astype(BF16)
        low = (rest - middle.astype(F32)).astype(BF16)
        terms = jnp.concatenate([high, middle, low], axis=1)
        both = dot(terms, mat)
        return both[:, :cells], both[:, cells:], terms

    def across(which, terms):
        mat = ends_ref[which][:, : terms.shape[1]]
        return [lax.dot_general(mat, terms[row * span : (row + 1) * span], (((1,), (1,)), ((), ())),
                                preferred_element_type=F32) for row in range(rows)]

    fwd = fwd_ref[...].reshape(rows * span, cells)
    bwd = bwd_ref[...].reshape(rows * span, cells)
    lane = lax.broadcasted_iota(jnp.int32, fwd.shape, 1)
    relative, absolute, terms = gathered(fwd, logs_ref[0])
    fwd_ends = across(0, terms)
    win_ref[...] = ((1.0 - fwd) * jnp.exp(-relative)).reshape(rows, span, cells)
    rf_ref[...] = jnp.exp(relative).reshape(rows, span, cells)
    entered = jnp.exp(absolute)
    relative, absolute, terms = gathered(bwd, logs_ref[1])
    bwd_ends = across(1, terms)
    grow = jnp.exp(relative)
    keep = jnp.where((lane == cells - 1) & (last_ref[0] == 1), 1.0, 1.0 - bwd)
    weight = keep * jnp.exp(-relative)
    wout_ref[...] = weight.reshape(rows, span, cells)
    rb_ref[...] = grow.reshape(rows, span, cells)
    tail_ref[...] = jnp.exp(absolute).reshape(rows, span, cells)
    high, low = parted(entered * weight)
    terms = jnp.concatenate([high, low], axis=1)
    carry_ref[...] = (grow * dot(terms, sums_ref[...])).reshape(rows, span, cells)
    carry_ends = across(2, terms)
    gains_ref[...] = jnp.zeros_like(gains_ref)
    for row in range(rows):
        ends_f, ends_b = jnp.exp(fwd_ends[row]), jnp.exp(bwd_ends[row])
        gains = (ends_f[0:1], ends_b[0:1], carry_ends[row][0:1] * ends_b[1:2], ends_f[1:2],
                 ends_b[1:2])
        for at, gain in enumerate(gains):
            gains_ref[at, row, :, :span] = gain


def sweep_kernel(rows, smooth_ref, mixed_ref, wall_ref, sums_ref, mine_ref,
                 recv_ref, u_ref, w_ref, win_ref, rf_ref, wout_ref, rb_ref, out_ref, last_ref,
                 first_ref, us_ref, ws_ref):
    tile = u_ref.shape[1]
    cells = u_ref.shape[2]
    fields, half = mine_ref.shape[1], mine_ref.shape[2]
    span = 2 * half
    lines = fields * rows
    at = pl.program_id(0)

    @pl.when(at == 0)
    def _():
        us_ref[pl.ds(6 * fields * span, us_ref.shape[0] - 6 * fields * span), :] = jnp.zeros(
            (us_ref.shape[0] - 6 * fields * span, cells), F32)
        ws_ref[pl.ds(2 * fields * span, ws_ref.shape[0] - 2 * fields * span), :] = jnp.zeros(
            (ws_ref.shape[0] - 2 * fields * span, cells), F32)
        last_ref[...] = jnp.zeros_like(last_ref)
        first_ref[...] = jnp.zeros_like(first_ref)
        first_core = lax.axis_index("yz") % 2 == 0

        def state(k):
            mine, recv = mine_ref[k], recv_ref[k]
            both = [jnp.where(first_core, mine, recv), jnp.where(first_core, recv, mine)]
            return jnp.concatenate(both, axis=1).reshape(fields * span, cells)

        for pair in ((0, 3), (1, 2), (4, 5)):
            wide = jnp.concatenate([state(k) for k in pair], axis=1)
            for field in range(fields):
                part = slice(field * span, (field + 1) * span)
                smooth = dot(smooth_ref[...], stacked(wide[part]))
                for place, k in enumerate(pair):
                    us_ref[pl.ds((k * fields + field) * span, span), :] = smooth[
                        :, place * cells : (place + 1) * cells
                    ]
            if pair == (0, 3):
                mixed = dot(mixed_ref[...], stacked(padded(wide, mixed_ref.shape[1] // 3)))
                for place in range(2):
                    ws_ref[pl.ds(place * fields * span, fields * span), :] = mixed[
                        :, place * cells : (place + 1) * cells
                    ]

    u_flat = u_ref.reshape(lines * tile, cells)
    w_flat = w_ref.reshape(lines * tile, cells)
    out_flat = out_ref.reshape(lines * tile, cells)
    rate_flat = [ref.reshape(rows * tile, cells) for ref in (win_ref, rf_ref, wout_ref, rb_ref)]
    lane = lax.broadcasted_iota(jnp.int32, (lines, last_ref.shape[1]), 1)
    last, first = last_ref[...], first_ref[...]
    rates = [
        jnp.concatenate([
            value for z in range(tile) for value in [ref[pl.ds(z, rows, stride=tile), :]] * fields], 0)
        for ref in rate_flat
    ]
    rights = []
    for z in range(0, tile, 2):
        wide = []
        for zz in (z, z + 1):
            where = at * tile + zz
            wide.append(jnp.concatenate([
                u_flat[pl.ds(zz, lines, stride=tile), :],
                us_ref[pl.ds(where, us_ref.shape[0] // span, stride=span), :],
                w_flat[pl.ds(zz, lines, stride=tile), :],
                ws_ref[pl.ds(where, ws_ref.shape[0] // span, stride=span), :]], 0))
        right = dot(wall_ref[...], stacked(jnp.concatenate(wide, 1)))
        rights += [right[:, :cells], right[:, cells:]]
    ahead = running(jnp.concatenate(rights, 0) * rates[0], sums_ref[0])
    ahead, total = ahead[:, :cells] * rates[1], ahead[:, cells:]
    result = running(ahead * rates[2], sums_ref[1])
    result, total_back = result[:, :cells] * rates[3], result[:, cells:]
    for z in range(tile):
        part = slice(z * lines, (z + 1) * lines)
        here = lane == at * tile + z
        out_flat[pl.ds(z, lines, stride=tile), :] = result[part]
        last = jnp.where(here, total[part], last)
        first = jnp.where(here, total_back[part], first)
    last_ref[...] = last
    first_ref[...] = first


def close_kernel(carry_ref, tail_ref, enter_ref, back_ref, t_ref, out_ref):
    fields, rows, span, _ = t_ref.shape
    for field in range(fields):
        enter = enter_ref[field].T[:span]
        back = back_ref[field].T[:span]
        for row in range(rows):
            out_ref[field, row] = (
                t_ref[field, row]
                + carry_ref[row] * enter[:, row : row + 1]
                + tail_ref[row] * back[:, row : row + 1]
            )


def params(limit):
    return pltpu.CompilerParams(vmem_limit_bytes=limit * 2**20)


def cost(flops, moved):
    return pl.CostEstimate(flops=int(flops), bytes_accessed=int(moved), transcendentals=0)


def whole(memory=pltpu.VMEM):
    return pl.BlockSpec(memory_space=memory)


SMEM = whole(pltpu.SMEM)


def shards(fields, inflow, rates_fwd, rates_bwd, flux_wall, flux_span, viscosity):
    n_fields, rows, span, cells = fields.shape
    devs, sections = lax.axis_size("yz"), lax.axis_size("gx")
    me, section = lax.axis_index("yz"), lax.axis_index("gx")
    chips, half = devs // 2, span // 2
    lines = n_fields * rows
    taps, local, reach, *maps = wall_tables(rows * devs, devs)
    flat = lambda table: jnp.asarray(np.asarray(table, np.float32).reshape(-1))
    taps, chip_mix, from_chip, to_core = (flat(table) for table in (taps, *maps))
    f32 = lambda table: jnp.asarray(np.asarray(table, np.float32))
    span_ops = operators(span, True)
    wall_ops, wall_pick, n_us, n_ws = wall_layout(local, reach, n_fields)
    width = wall_pick.shape[1]
    span_width = -(-n_fields * span // 128) * 128
    pad = lambda mat: np.pad(mat, [(0, 0)] * (mat.ndim - 1) + [(0, span_width - n_fields * span)])
    size = 8
    up_to = lambda mat: np.pad(mat, ((0, size - n_fields), (0, 0)))
    span_cols = pad(np.repeat(np.eye(n_fields), span, axis=1))
    tiny = jnp.zeros((3 * size, size), F32)
    tiny = lax.dynamic_update_slice(tiny, flux_wall, (0, 0))
    tiny = lax.dynamic_update_slice(tiny, flux_span, (size, 0))
    tiny = lax.dynamic_update_slice(tiny, viscosity[None], (2 * size, 0))
    smooth_mat = jnp.asarray(split(span_ops[0]))
    dev_block = lambda *shape: pl.BlockSpec(
        (1, *shape), lambda i, dev: (dev[0],) + (0,) * len(shape))
    full_block = lambda *shape: pl.BlockSpec(shape, lambda i, dev: (0,) * len(shape))
    all_span = n_fields * span
    wall_mat, mixed_mat = pl.pallas_call(
        mats_kernel,
        grid_spec=pltpu.PrefetchScalarGridSpec(
            num_scalar_prefetch=1,
            grid=(1,),
            in_specs=[
                pl.BlockSpec((size, size), lambda i, dev: (0, 0)),
                pl.BlockSpec((size, size), lambda i, dev: (1, 0)),
                pl.BlockSpec((size, size), lambda i, dev: (2, 0)),
                full_block(size, width), dev_block(3, rows, width), full_block(size, span_width),
                full_block(3, span, span_width)],
            out_specs=[full_block(lines, 3 * width), full_block(all_span, 3 * span_width)],
        ),
        out_shape=[
            jax.ShapeDtypeStruct((lines, 3 * width), BF16),
            jax.ShapeDtypeStruct((all_span, 3 * span_width), BF16)],
        compiler_params=params(LIMITS["mats"]),
        cost_estimate=cost(10**7, 8 * 10**6),
        name="mats",
    )(me.astype(jnp.int32).reshape(1), tiny, tiny, tiny, f32(up_to(wall_pick)),
      f32(wall_ops), f32(up_to(span_cols)),
      f32(np.stack([pad(np.tile(span_ops[k], (1, n_fields))) for k in (1, 2, 0)])))
    tri = np.triu(np.ones((cells, cells), np.float32))
    ones = np.ones_like(tri)
    twice = lambda mat: np.concatenate([mat, mat], 0)
    sums = jnp.asarray(np.stack([
        twice(np.concatenate([tri, ones], 1)), twice(np.concatenate([tri.T, ones], 1))
    ])).astype(BF16)
    logs_fwd = tri - tri[:, cells // 2 - 1 :][:, :1]
    logs_bwd = tri.T - tri.T[:, cells // 2 :][:, :1]
    thrice = lambda mat: np.concatenate([mat, mat, mat], 0)
    logs = jnp.asarray(np.stack([
        thrice(np.concatenate([logs_fwd, tri], 1)), thrice(np.concatenate([logs_bwd, tri.T], 1))
    ])).astype(BF16)

    tap_shape = jax.ShapeDtypeStruct((6, n_fields, half, cells), F32)
    tap_block = pl.BlockSpec((6, 1, half, cells), lambda f: (0, f, 0, 0))
    keep, send = pl.pallas_call(
        taps_kernel,
        grid=(n_fields,),
        in_specs=[SMEM, pl.BlockSpec((1, rows, span, cells), lambda f: (f, 0, 0, 0))],
        out_specs=[tap_block, tap_block],
        out_shape=[tap_shape, tap_shape],
        compiler_params=params(LIMITS["taps"]),
        cost_estimate=cost(12 * fields.size, 4 * fields.size),
        name="taps",
    )(taps, fields)
    swap_cores = [(dev, dev ^ 1) for dev in range(devs)]
    tap_lines = n_fields * half
    keep = keep.reshape(6, tap_lines, cells)
    other = lax.ppermute(send.reshape(6, tap_lines, cells), "yz", swap_cores)
    part_shape = jax.ShapeDtypeStruct((3, tap_lines, cells), F32)
    outgoing = pl.pallas_call(
        functools.partial(chip_kernel, chips),
        in_specs=[SMEM, whole(), whole()],
        out_specs=[whole()] * (chips - 1),
        out_shape=[part_shape] * (chips - 1),
        compiler_params=params(LIMITS["chip"]),
        cost_estimate=cost(6 * keep.size, 12 * keep.size),
        name="chip",
    )(chip_mix, keep, other)
    held_fields, held_fwd, held_bwd, wall_mat, mixed_mat, *outgoing = lax.optimization_barrier(
        (fields, rates_fwd, rates_bwd, wall_mat, mixed_mat, *outgoing))
    arrived = [
        lax.ppermute(value, "yz", [(dev, dev ^ (2 * (at + 1))) for dev in range(devs)])
        for at, value in enumerate(outgoing)
    ]
    n_span = 4
    pair_block = pl.BlockSpec((n_fields, n_span, span, cells), lambda i: (0, i, 0, 0))
    field_shape = jax.ShapeDtypeStruct(fields.shape, F32)
    smooth, mixed = pl.pallas_call(
        span_kernel,
        grid=(rows // n_span,),
        in_specs=[whole(), whole(), pair_block],
        out_specs=[pair_block, pair_block],
        out_shape=[pltpu.HBM(fields.shape, F32)] * 2,
        compiler_params=params(LIMITS["span"]),
        cost_estimate=cost(2 * 4000 * fields.size, 12 * fields.size),
        name="span",
    )(smooth_mat, mixed_mat, held_fields)

    n_rate = 8
    rate_block = pl.BlockSpec((n_rate, span, cells), lambda i: (i, 0, 0))
    rate_shape = jax.ShapeDtypeStruct(rates_fwd.shape, F32)
    is_last = (section == sections - 1).astype(jnp.int32).reshape(1)
    lanes = -(-span // 128) * 128
    widen = lambda value: jnp.pad(value, [(0, 0)] * (value.ndim - 1) + [(0, lanes - span)])
    ends = np.zeros((3, 16, 3 * cells))
    ends[:, 0] = 1.0
    ends[0, 1] = np.tile(np.arange(cells) >= cells // 2, 3)
    ends[1, 1] = np.tile(np.arange(cells) < cells // 2, 3)
    *rate_parts, carry, tail, gains = pl.pallas_call(
        rates_kernel,
        grid=(rows // n_rate,),
        in_specs=[SMEM, whole(), whole(), whole(), rate_block, rate_block],
        out_specs=[rate_block] * 6 + [pl.BlockSpec((5, n_rate, 1, lanes), lambda i: (0, i, 0, 0))],
        out_shape=[pltpu.HBM(rates_fwd.shape, F32)] * 6 + [jax.ShapeDtypeStruct((5, rows, 1, lanes), F32)],
        compiler_params=params(LIMITS["rates"]),
        cost_estimate=cost(2 * 4000 * rates_fwd.size, 32 * rates_fwd.size),
        name="rates",
    )(is_last, logs, sums[1, :, :cells], jnp.asarray(ends.astype(BF16)), held_fwd, held_bwd)
    smooth, mixed, gains, *arrived = lax.optimization_barrier((smooth, mixed, gains, *arrived))
    six_shape = jax.ShapeDtypeStruct((6, tap_lines, cells), F32)
    mine, theirs = pl.pallas_call(
        functools.partial(states_kernel, chips),
        in_specs=[SMEM] * 2 + [whole()] * (chips + 1),
        out_specs=[whole()] * 2,
        out_shape=[six_shape] * 2,
        compiler_params=params(LIMITS["states"]),
        cost_estimate=cost(20 * keep.size, 20 * keep.size),
        name="states",
    )(from_chip, to_core, keep, other, *arrived)
    recv = lax.ppermute(theirs, "yz", swap_cores)
    recv, gains = lax.optimization_barrier((recv, gains.reshape(5, rows, lanes)))
    end_fwd, end_bwd = gains[3], gains[4]
    gains = gains[:3]
    others = [
        lax.ppermute(gains, "gx", [(at, at ^ hop) for at in range(sections)])
        for hop in range(1, sections)
    ]
    arrivals = jnp.stack([gains] + others)
    every = jnp.stack([
        lax.dynamic_index_in_dim(arrivals, section ^ at, 0, False)
        for at in range(sections)
    ])
    gain_f, gain_b, gain_c = every[:, 0], every[:, 1], every[:, 2]
    turned = [None] * sections
    turned[sections - 1] = jnp.zeros_like(gain_f[0])
    for at in range(sections - 2, -1, -1):
        turned[at] = gain_c[at + 1] + gain_b[at + 1] * gain_f[at + 1] * turned[at + 1]
    own = lambda value: lax.dynamic_index_in_dim(value, section, 0, False)
    turn = own(jnp.stack(turned))
    turn_out = own(gain_b) * turn
    start_gain, hop_fwd, hop_bwd = [], [], []
    one, zero = jnp.ones_like(gain_f[0]), jnp.zeros_like(gain_f[0])
    for to in range(sections):
        value = one
        for at in range(to):
            value = value * gain_f[at]
        start_gain.append(value)
        fwd_row, bwd_row = [], []
        for hop in range(1, sections):
            source = to ^ hop
            value = one
            for at in range(min(source, to) + 1, max(source, to)):
                value = value * (gain_f if source < to else gain_b)[at]
            fwd_row.append(value if source < to else zero)
            bwd_row.append(value if source > to else zero)
        hop_fwd.append(jnp.stack(fwd_row))
        hop_bwd.append(jnp.stack(bwd_row))
    entering = own(jnp.stack(start_gain))[None] * widen(inflow)
    hop_fwd, hop_bwd = own(jnp.stack(hop_fwd)), own(jnp.stack(hop_bwd))
    own_gain = own(gain_f)

    tile = 8
    line_block = pl.BlockSpec((lines, tile, cells), lambda i: (0, i, 0))
    rate_tile = pl.BlockSpec((rows, tile, cells), lambda i: (0, i, 0))
    end_block = pl.BlockSpec((lines, lanes), lambda i: (0, 0))
    end_shape = jax.ShapeDtypeStruct((lines, lanes), F32)
    as_lines = lambda value: value.reshape(lines, span, cells)
    as_states = lambda value: value.reshape(6, n_fields, half, cells)
    swept, last, first = pl.pallas_call(
        functools.partial(sweep_kernel, rows),
        grid=(span // tile,),
        in_specs=[whole()] * 6 + [line_block] * 2 + [rate_tile] * 4,
        out_specs=[line_block, end_block, end_block],
        out_shape=[pltpu.VMEM((lines, span, cells), F32), end_shape, end_shape],
        scratch_shapes=[
            pltpu.VMEM((n_us * span, cells), F32), pltpu.VMEM((n_ws * span, cells), F32)],
        compiler_params=params(LIMITS["sweep"]),
        cost_estimate=cost(2 * 3000 * fields.size, 12 * fields.size),
        name="sweep",
    )(smooth_mat, mixed_mat, wall_mat, sums, as_states(mine), as_states(recv),
      as_lines(smooth), as_lines(mixed), *rate_parts)
    last = last.reshape(n_fields, rows, lanes) * end_fwd[None]
    first = first.reshape(n_fields, rows, lanes) * end_bwd[None]

    upstream = first + turn_out[None] * last
    back = jnp.zeros_like(last)
    for hop in range(1, sections):
        payload = jnp.where((section ^ hop) > section, last, upstream)
        got = lax.ppermute(payload, "gx", [(at, at ^ hop) for at in range(sections)])
        entering = entering + hop_fwd[hop - 1][None] * got
        back = back + hop_bwd[hop - 1][None] * got
    back = back + turn[None] * (own_gain[None] * entering + last)

    n_close = 8
    close_block = pl.BlockSpec((n_fields, n_close, span, cells), lambda i: (0, i, 0, 0))
    gain_block = pl.BlockSpec((n_close, span, cells), lambda i: (i, 0, 0))
    state_block = pl.BlockSpec((n_fields, n_close, lanes), lambda i: (0, i, 0))
    return pl.pallas_call(
        close_kernel,
        grid=(rows // n_close,),
        in_specs=[gain_block, gain_block, state_block, state_block, close_block],
        out_specs=close_block,
        out_shape=field_shape,
        compiler_params=params(LIMITS["close"]),
        cost_estimate=cost(4 * fields.size, 10 * fields.size),
        name="close",
    )(carry, tail, entering, back, swept.reshape(fields.shape))


def solution(mesh):
    placed = (
        P(None, "yz", None, "gx"), P(None, "yz", None), P("yz", None, "gx"), P("yz", None, "gx"),
        P(), P(), P(),
    )
    return jax.shard_map(
        shards, mesh=mesh, in_specs=placed, out_specs=P(None, "yz", None, "gx"), check_vma=False
    )
```
